256 devices in a mesh: ctx: 32 (over z, y), tp: 8 (over x, core).
Axes of the slice: x: 4, y: 4, z: 8, core: 2. Of those that a mesh axis runs over, the one named last changes fastest.
Arguments:
- queries: bfloat16 [512, 128, 576], P('ctx', 'tp'), may hold values from -20 to 20
- latent_cache: bfloat16 [1024, 64, 576], P('ctx'), may hold values from -6 to 6
- output_gradient: bfloat16 [512, 128, 512], P('ctx', 'tp'), may hold values from -6 to 6
- selected: int32 [512, 32], P('ctx'), may hold values from 0 to 1023, as said below
- positions: int32 [512], P('ctx'), may hold values from 63488 to 65535, as said below
Outputs:
- attended: bfloat16 [512, 128, 512], P('ctx', 'tp')
- query_grad: bfloat16 [512, 128, 576], P('ctx', 'tp')
- cache_grad: bfloat16 [1024, 64, 576], P('ctx', 'tp')
The draws below stay inside these ranges and needn't reach their ends.
Inputs may be any that keep to these rules, and one draw needn't show every extreme that they name: `selected`: each row names 32 different blocks; its last entry is the block that holds the row's position, one of the last 32 blocks, and the others lie in the first 992 blocks. The rows of one ctx index name exactly 64 different blocks together, and at most 3 of them lie in the blocks of any one ctx index. The queries of one ctx index hold consecutive positions, in order, inside one block.
All inputs are finite; a program needn't handle non-finite values.
Results may differ from the reference program's by a relative error of at most 0.028.
Values may be sent and summed in bfloat16 or wider, within the bound.
No kernel may reach another device: no remote copies, remote signals or barrier semaphores. Data moves between devices by JAX's collectives and lax.ppermute only.
A program may use at most 128 MiB of HBM per device.

```python
import jax
import jax.numpy as jnp
from jax import lax

HEAD_TOTAL = 128
LATENT_WIDTH = 512
ROTARY_WIDTH = 64
BT = 64
TOPB = 32
USED = 64
BLK_DEV = 32
QRY_DEV = 16
QK = 576
COLD = 31
CAP = 3
QUERY_TOTAL = 512
NBLK = 1024
N_CTX = 32


def routing_draw(key):
    key = jax.random.fold_in(key, 11)
    keys_list = jax.random.split(key, 5)
    extra_count = USED - 1 - COLD
    extra_slots = COLD * (CAP - 1)
    owner_of = jnp.repeat(jnp.arange(COLD, dtype=jnp.int32), CAP - 1)
    slot_noise = jax.random.randint(keys_list[0], (N_CTX, extra_slots), 0, 2 * COLD)
    ranking = (slot_noise + owner_of[None, :]) * extra_slots + jnp.arange(extra_slots, dtype=jnp.int32)[None, :]
    slot_order = jnp.argsort(-ranking, axis=1).astype(jnp.int32)
    row_ids = jnp.arange(N_CTX, dtype=jnp.int32)[:, None]
    taken_slots = jnp.zeros((N_CTX, extra_slots), jnp.int32).at[row_ids, slot_order[:, :extra_count]].set(1)
    counts = 1 + taken_slots.reshape(N_CTX, COLD, CAP - 1).sum(axis=2)
    local_noise = jax.random.randint(keys_list[1], (N_CTX, COLD, BLK_DEV), 0, 1 << 20) * BLK_DEV + jnp.arange(BLK_DEV, dtype=jnp.int32)
    local_order = jnp.argsort(local_noise, axis=2)[:, :, :CAP].astype(jnp.int32)
    level_ids = jnp.arange(CAP, dtype=jnp.int32)
    valid_slot = level_ids[None, None, :] < counts[:, :, None]
    global_ids = jnp.arange(COLD, dtype=jnp.int32)[None, :, None] * BLK_DEV + local_order
    flat_valid = valid_slot.reshape(N_CTX, COLD * CAP)
    flat_ids = global_ids.reshape(N_CTX, COLD * CAP)
    rank_ids = jnp.cumsum(flat_valid.astype(jnp.int32), axis=1) - 1
    target = jnp.where(flat_valid, rank_ids, USED - 1)
    pool_ids = jnp.zeros((N_CTX, USED - 1), jnp.int32).at[row_ids, target].set(flat_ids, mode='drop')
    shuffle_noise = jax.random.randint(keys_list[2], (N_CTX, USED - 1), 0, 1 << 20) * (USED - 1) + jnp.arange(USED - 1, dtype=jnp.int32)
    shuffled = jnp.take_along_axis(pool_ids, jnp.argsort(shuffle_noise, axis=1).astype(jnp.int32), axis=1)
    own_block = COLD * BLK_DEV + jax.random.randint(keys_list[3], (N_CTX,), 0, BLK_DEV)
    offset = jax.random.randint(keys_list[4], (N_CTX,), 0, BT - QRY_DEV + 1)
    start_pos = own_block * BT + offset
    positions = (start_pos[:, None] + jnp.arange(QRY_DEV, dtype=jnp.int32)[None, :]).reshape(QUERY_TOTAL)
    window_ids = (jnp.arange(QRY_DEV, dtype=jnp.int32)[:, None] * (TOPB - 1) + jnp.arange(TOPB - 1, dtype=jnp.int32)[None, :]) % (USED - 1)
    pool_picks = shuffled[:, window_ids]
    own_column = jnp.broadcast_to(own_block[:, None, None], (N_CTX, QRY_DEV, 1))
    selected = jnp.concatenate([pool_picks, own_column], axis=2).reshape(QUERY_TOTAL, TOPB)
    return (selected.astype(jnp.int32), positions.astype(jnp.int32))


def cache_base(key):
    key = jax.random.fold_in(key, 29)
    return jax.random.normal(key, (NBLK, BT, QK), jnp.float32)


def draw_selected(key, part):
    routing = routing_draw(key)
    return routing[0]


def draw_positions(key, part):
    routing = routing_draw(key)
    return routing[1]


def draw_latent_cache(key, part):
    base_values = cache_base(key)
    return jnp.clip(base_values, -6.0, 6.0).astype(jnp.bfloat16)


def draw_queries(key, part):
    key = jax.random.fold_in(key, 5)
    return jnp.clip(jax.random.normal(key, (QUERY_TOTAL, HEAD_TOTAL, QK), jnp.float32) * 1.5, -9.0, 9.0).astype(jnp.bfloat16)


def levels(key, extent, cuts, low, top_value):
    factor_of = 1.0
    for dim, blocks in cuts:
        draws = jax.random.uniform(jax.random.fold_in(jax.random.fold_in(key, 6), dim), (blocks,), jnp.float32, low / len(cuts), top_value / len(cuts))
        factor_of = factor_of * jnp.repeat(jnp.exp(draws), extent[dim] // blocks).reshape((-1,) + (1,) * (len(extent) - 1 - dim))
    return factor_of


def bell_draw(key, extent, spread, most, shards=(), kind=jnp.bfloat16):
    entries = jax.random.normal(key, extent, jnp.float32) * spread
    if len(shards) > 0:
        entries = levels(key, extent, shards, -0.22, 0.18) * entries
    return jnp.clip(entries, min=-most, max=most).astype(kind)


def setup_inputs(seed: int = 0) -> dict:
    streams_of = jax.random.split(jax.random.key(seed), 6)
    return {
        "queries": draw_queries(jax.random.fold_in(streams_of[5], 71), 0),
        "latent_cache": draw_latent_cache(jax.random.fold_in(streams_of[5], 71), 0),
        "output_gradient": bell_draw(streams_of[2], (QUERY_TOTAL, HEAD_TOTAL, LATENT_WIDTH), 1.0, 6.0, ((0, 32), (1, 8))),
        "selected": draw_selected(jax.random.fold_in(streams_of[5], 71), 0),
        "positions": draw_positions(jax.random.fold_in(streams_of[5], 71), 0),
    }


score_scale = 192.0 ** -0.5


def reference(queries, latent_cache, output_gradient, selected, positions):
    entire_width = LATENT_WIDTH + ROTARY_WIDTH

    def per_query(totals, inputs_row):
        query_row, grad_row, block_ids, position = inputs_row
        block_ids = block_ids.astype(jnp.int32)
        key_matrix = latent_cache[block_ids].reshape(TOPB * BT, entire_width)
        token_pos = (block_ids[:, None] * BT + jnp.arange(BT, dtype=jnp.int32)[None, :]).reshape(TOPB * BT)
        visible = token_pos <= position
        scores = jnp.dot(query_row, key_matrix.T, preferred_element_type=jnp.float32) * score_scale
        scores = jnp.where(visible[None, :], scores, -jnp.inf)
        peak_score = jnp.max(scores, axis=1, keepdims=True)
        exponent = jnp.exp(scores - peak_score)
        weights = exponent / jnp.sum(exponent, axis=1, keepdims=True)
        weight_half = weights.astype(jnp.bfloat16)
        value_matrix = key_matrix[:, :LATENT_WIDTH]
        attended = jnp.dot(weight_half, value_matrix, preferred_element_type=jnp.float32)
        grad_weights = jnp.dot(grad_row, value_matrix.T, preferred_element_type=jnp.float32)
        row_inner = jnp.sum(weights * grad_weights, axis=1, keepdims=True)
        score_half = (weights * (grad_weights - row_inner)).astype(jnp.bfloat16)
        query_grad = jnp.dot(score_half, key_matrix, preferred_element_type=jnp.float32) * score_scale
        key_grad = jnp.dot(score_half.T, query_row, preferred_element_type=jnp.float32) * score_scale
        value_grad = jnp.dot(weight_half.T, grad_row, preferred_element_type=jnp.float32)
        key_grad = key_grad + jnp.pad(value_grad, ((0, 0), (0, ROTARY_WIDTH)))
        totals = totals.at[block_ids].add(key_grad.reshape(TOPB, BT, entire_width))
        return totals, (attended.astype(jnp.bfloat16), query_grad.astype(jnp.bfloat16))

    initial = jnp.zeros((NBLK, BT, entire_width), jnp.float32)
    total_grad, (attended_all, query_all) = lax.scan(per_query, initial, (queries, output_gradient, selected, positions))
    return attended_all, query_all, total_grad.astype(jnp.bfloat16)
```

```python
import functools
import math

import jax
import jax.numpy as jnp
from jax import lax
from jax.experimental import pallas as pl
from jax.experimental.pallas import tpu as pltpu
from jax.sharding import PartitionSpec as P

USED = 64
XN = 4
CORES = 2

score_scale = 192.0 ** (-0.5)
log2e = 1.0 / math.log(2.0)
VMEM_LIMIT = 48 * 1024 * 1024
bf16 = jnp.bfloat16
f32 = jnp.float32


def x_shift(k):
    return [
        (x * CORES + c, ((x + k) % XN) * CORES + c) for x in range(XN) for c in range(CORES)
    ]


CORE_SWAP = [(t, t ^ 1) for t in range(XN * CORES)]


def send_x(value, k):
    return lax.ppermute(value, "tp", x_shift(k % XN))


def nt_dot(a, b):
    return lax.dot_general(a, b, (((1,), (1,)), ((), ())), preferred_element_type=f32)


def score_kernel(bias_ref, own_ref, other_ref, *refs):
    q_refs, g_refs = refs[:XN], refs[XN : 2 * XN]
    p_ref, gw_ref, stat_ref = refs[2 * XN :]
    half, width = own_ref.shape
    value_width = g_refs[0].shape[1]
    step = pl.program_id(0)
    for k in range(XN):

        @pl.when(step == k)
        def _(k=k):
            q, g = q_refs[k][...], g_refs[k][...]
            scores = []
            for h, key_ref in enumerate((own_ref, other_ref)):
                s = nt_dot(key_ref[...], q) * (score_scale * log2e)
                scores.append(s + bias_ref[h * half : (h + 1) * half, :].astype(f32))
            peak = jnp.maximum(
                jnp.max(scores[0], axis=0, keepdims=True), jnp.max(scores[1], axis=0, keepdims=True)
            )
            total = jnp.zeros_like(peak)
            inner = jnp.zeros_like(peak)
            for h, key_ref in enumerate((own_ref, other_ref)):
                p = jnp.exp2(scores[h] - peak)
                gw = nt_dot(key_ref[:, :value_width], g)
                total += jnp.sum(p, axis=0, keepdims=True)
                inner += jnp.sum(p * gw, axis=0, keepdims=True)
                p_ref[0, h * half : (h + 1) * half, :] = p.astype(bf16)
                gw_ref[0, h * half : (h + 1) * half, :] = gw
            stat_ref[0, 0:1, :] = peak
            stat_ref[0, 1:2, :] = total
            stat_ref[0, 2:3, :] = inner
            stat_ref[0, 3:8, :] = jnp.zeros((5, peak.shape[1]), f32)


def key_grad_kernel(p_ref, gw_ref, *refs):
    stat_refs, q_refs, g_refs = refs[:XN], refs[XN : 2 * XN], refs[2 * XN : 3 * XN]
    w_ref, ds_ref, own_ref, other_ref, acc_ref = refs[3 * XN :]
    half = own_ref.shape[0]
    value_width = g_refs[0].shape[1]
    step = pl.program_id(0)
    for k in range(XN):

        @pl.when(step == k)
        def _(k=k):
            stats = [stat_refs[j][(k - j) % XN] for j in range(XN)]
            peak = functools.reduce(jnp.maximum, [s[0:1] for s in stats])
            factors = [jnp.exp2(s[0:1] - peak) for s in stats]
            total = sum(s[1:2] * f for s, f in zip(stats, factors))
            inner = sum(s[2:3] * f for s, f in zip(stats, factors)) / total
            factor = factors[0] / total
            weights = p_ref[0].astype(f32) * factor
            ds = (weights * (gw_ref[0] - inner) * score_scale).astype(bf16)
            w = weights.astype(bf16)
            w_ref[0] = w
            ds_ref[0] = ds
            grad = jnp.dot(ds, q_refs[k][...], preferred_element_type=f32)
            value_grad = jnp.dot(w, g_refs[k][...], preferred_element_type=f32)
            if k == 0:
                acc_ref[...] = grad
            else:
                acc_ref[...] += grad
            acc_ref[:, :value_width] += value_grad

    @pl.when(step == XN - 1)
    def _():
        own_ref[...] = acc_ref[:half, :]
        other_ref[...] = acc_ref[half:, :].astype(bf16)


def query_grad_kernel(own_ref, other_ref, w_ref, ds_ref, *refs):
    out_refs, keys_t = refs[:XN], refs[XN]
    half, width = own_ref.shape
    value_width = out_refs[0].shape[0] - width
    step = pl.program_id(0)

    @pl.when(step == 0)
    def _():
        keys_t[:, :half] = own_ref[...].T
        keys_t[:, half:] = other_ref[...].T

    for k in range(XN):

        @pl.when(step == k)
        def _(k=k):
            att = jnp.dot(keys_t[:value_width, :], w_ref[0], preferred_element_type=f32)
            qg = jnp.dot(keys_t[...], ds_ref[0], preferred_element_type=f32)
            out_refs[k][:value_width, :] = att.astype(bf16)
            out_refs[k][value_width:, :] = qg.astype(bf16)


def combine_kernel(*refs):
    parts, att_ref, qg_ref = refs[:XN], refs[XN], refs[XN + 1]
    value_width = att_ref.shape[1]
    total = sum(part[...].astype(f32) for part in parts)
    att_ref[...] = total[:value_width].astype(bf16).T
    qg_ref[...] = total[value_width:].astype(bf16).T


def whole(shape):
    return pl.BlockSpec(shape, lambda i: (0,) * len(shape))


def params():
    return pltpu.CompilerParams(vmem_limit_bytes=VMEM_LIMIT)


def slot_table(selected, block_count, owners, slot_limit):
    block_range = jnp.arange(owners * block_count, dtype=jnp.int32)
    wanted = jnp.any(selected.reshape(-1)[:, None] == block_range[None, :], axis=0)
    wanted = wanted.reshape(owners, block_count)
    rank_within = jnp.cumsum(wanted.astype(jnp.int32), axis=1) - 1
    local_ids = jnp.arange(block_count, dtype=jnp.int32)
    slot_range = jnp.arange(slot_limit, dtype=jnp.int32)
    matches = wanted[:, None, :] & (rank_within[:, None, :] == slot_range[None, :, None])
    present = jnp.any(matches, axis=2)
    found_ids = jnp.sum(jnp.where(matches, local_ids[None, None, :], 0), axis=2)
    return jnp.where(present, found_ids, -1)


def row_targets(ids, tokens):
    token = jnp.arange(tokens, dtype=jnp.int32)
    rows = jnp.where(ids[:, None] >= 0, ids[:, None] * tokens + token[None, :], -1)
    return rows.reshape(-1)


def on_device(queries, latent_cache, output_gradient, selected, positions):
    query_count, head_count, width = queries.shape
    block_count, block_size, _ = latent_cache.shape
    value_width = output_gradient.shape[2]
    owners = lax.axis_size("ctx")
    tp = lax.axis_index("tp")
    tokens = block_size // (XN * CORES)
    slot_limit = (USED - 2) // (owners - 1) + 1
    slots = owners * slot_limit
    rows = query_count * head_count
    half = USED * tokens
    keys = CORES * half

    requests = slot_table(selected, block_count, owners, slot_limit)
    asked_ids = lax.all_to_all(requests, "ctx", split_axis=0, concat_axis=0, tiled=True)

    query_rows = queries.reshape(rows, width)
    grad_rows = output_gradient.reshape(rows, value_width)
    q_parts = [query_rows] + [send_x(query_rows, k) for k in range(1, XN)]
    g_parts = [grad_rows] + [send_x(grad_rows, k) for k in range(1, XN)]

    my_tokens = lax.dynamic_slice_in_dim(latent_cache, tp * tokens, tokens, axis=1)
    my_tokens = my_tokens.reshape(block_count * tokens, width)
    asked_rows = row_targets(asked_ids.reshape(-1), tokens)
    asked_hot = (
        asked_rows[:, None] == jnp.arange(block_count * tokens, dtype=jnp.int32)[None, :]
    ).astype(bf16)
    packed = jnp.dot(asked_hot, my_tokens, preferred_element_type=f32).astype(bf16)
    fetched = lax.all_to_all(
        packed.reshape(owners, slot_limit * tokens, width), "ctx", 0, 0, tiled=True
    ).reshape(slots * tokens, width)

    flat_requests = requests.reshape(-1)
    used_slot = flat_requests >= 0
    slot_order = jnp.where(used_slot, jnp.cumsum(used_slot.astype(jnp.int32)) - 1, -1)
    compact = jnp.arange(USED, dtype=jnp.int32)
    slot_match = slot_order[None, :] == compact[:, None]
    slot_owner = jnp.arange(slots, dtype=jnp.int32) // slot_limit
    slot_block = slot_owner * block_count + flat_requests
    block_ids = jnp.sum(jnp.where(slot_match, slot_block[None, :], 0), axis=1)
    slot_rows = row_targets(slot_order, tokens)
    spread_hot = (slot_rows[:, None] == jnp.arange(half, dtype=jnp.int32)[None, :]).astype(bf16)

    chosen = jnp.any(selected[None, :, :] == block_ids[:, None, None], axis=2)
    token = jnp.arange(tokens, dtype=jnp.int32)
    token_pos = jnp.stack(
        [block_ids[:, None] * block_size + t * tokens + token[None, :] for t in (tp, tp ^ 1)]
    )
    visible = chosen[None, :, None, :] & (
        token_pos[:, :, :, None] <= positions[None, None, None, :]
    )
    bias = jnp.where(visible, 0.0, -jnp.inf).astype(bf16).reshape(keys, query_count)
    bias = jnp.broadcast_to(bias[:, :, None], (keys, query_count, head_count)).reshape(keys, rows)

    own_keys = lax.dot_general(
        spread_hot, fetched, (((0,), (0,)), ((), ())), preferred_element_type=f32
    ).astype(bf16)
    other_keys = lax.ppermute(own_keys, "tp", CORE_SWAP)

    blocked = pl.BlockSpec((1, keys, rows), lambda i: (i, 0, 0))
    p, gw, stats = pl.pallas_call(
        score_kernel,
        grid=(XN,),
        in_specs=[whole((keys, rows))]
        + [whole((half, width))] * 2
        + [whole((rows, width))] * XN
        + [whole((rows, value_width))] * XN,
        out_specs=[blocked, blocked, pl.BlockSpec((1, 8, rows), lambda i: (i, 0, 0))],
        out_shape=[
            jax.ShapeDtypeStruct((XN, keys, rows), bf16),
            jax.ShapeDtypeStruct((XN, keys, rows), f32),
            jax.ShapeDtypeStruct((XN, 8, rows), f32),
        ],
        compiler_params=params(),
        name="scores",
    )(bias, own_keys, other_keys, *q_parts, *g_parts)
    all_stats = [stats] + [send_x(stats, k) for k in range(1, XN)]

    w, ds, own_grad, other_grad = pl.pallas_call(
        key_grad_kernel,
        grid=(XN,),
        in_specs=[blocked, blocked]
        + [whole((XN, 8, rows))] * XN
        + [whole((rows, width))] * XN
        + [whole((rows, value_width))] * XN,
        out_specs=[blocked, blocked, whole((half, width)), whole((half, width))],
        out_shape=[
            jax.ShapeDtypeStruct((XN, keys, rows), bf16),
            jax.ShapeDtypeStruct((XN, keys, rows), bf16),
            jax.ShapeDtypeStruct((half, width), f32),
            jax.ShapeDtypeStruct((half, width), bf16),
        ],
        scratch_shapes=[pltpu.VMEM((keys, width), f32)],
        compiler_params=params(),
        name="key_grad",
    )(p, gw, *all_stats, *q_parts, *g_parts)
    from_core = lax.ppermute(other_grad, "tp", CORE_SWAP)

    parts = pl.pallas_call(
        query_grad_kernel,
        grid=(XN,),
        in_specs=[whole((half, width))] * 2 + [blocked, blocked],
        out_specs=[whole((width + value_width, rows))] * XN,
        out_shape=[jax.ShapeDtypeStruct((width + value_width, rows), bf16)] * XN,
        scratch_shapes=[pltpu.VMEM((width, keys), bf16)],
        compiler_params=params(),
        name="query_grad",
    )(own_keys, other_keys, w, ds)
    parts = [parts[0]] + [send_x(parts[k], -k) for k in range(1, XN)]

    block_grad = (own_grad + from_core.astype(f32)).astype(bf16)
    spread = jnp.dot(spread_hot, block_grad, preferred_element_type=f32).astype(bf16)
    returned = lax.all_to_all(
        spread.reshape(owners, slot_limit * tokens, width), "ctx", 0, 0, tiled=True
    ).reshape(slots * tokens, width)
    cache_grad = lax.dot_general(
        asked_hot, returned, (((0,), (0,)), ((), ())), preferred_element_type=f32
    ).astype(bf16)

    attended, query_grad = pl.pallas_call(
        combine_kernel,
        out_shape=[
            jax.ShapeDtypeStruct((rows, value_width), bf16),
            jax.ShapeDtypeStruct((rows, width), bf16),
        ],
        compiler_params=params(),
        name="combine",
    )(*parts)
    return (
        attended.reshape(query_count, head_count, value_width),
        query_grad.reshape(query_count, head_count, width),
        cache_grad.reshape(block_count, tokens, width),
    )


def solution(mesh):
    in_specs = (
        P("ctx", "tp", None),
        P("ctx", None, None),
        P("ctx", "tp", None),
        P("ctx", None),
        P("ctx"),
    )
    out_specs = (P("ctx", "tp", None), P("ctx", "tp", None), P("ctx", "tp", None))
    return jax.shard_map(
        on_device, mesh=mesh, in_specs=in_specs, out_specs=out_specs, check_vma=False
    )
```

```python
import functools
import math

import jax
import jax.numpy as jnp
from jax import lax
from jax.experimental import pallas as pl
from jax.experimental.pallas import tpu as pltpu
from jax.sharding import PartitionSpec as P

USED = 64
XN = 4
CORES = 2

score_scale = 192.0 ** (-0.5)
log2e = 1.0 / math.log(2.0)
VMEM_LIMIT = 24 * 1024 * 1024
bf16 = jnp.bfloat16
f32 = jnp.float32


def x_shift(k):
    return [
        (x * CORES + c, ((x + k) % XN) * CORES + c) for x in range(XN) for c in range(CORES)
    ]


CORE_SWAP = [(t, t ^ 1) for t in range(XN * CORES)]


def send_x(value, k):
    return lax.ppermute(value, "tp", x_shift(k % XN))


def nt_dot(a, b):
    return lax.dot_general(a, b, (((1,), (1,)), ((), ())), preferred_element_type=f32)


def expand(rows, tokens):
    count, lanes = rows.shape
    wide = jnp.broadcast_to(rows[:, None, :], (count, tokens, lanes))
    return wide.reshape(count * tokens, lanes)


def iotas(shape):
    return (lax.broadcasted_iota(jnp.int32, shape, 0), lax.broadcasted_iota(jnp.int32, shape, 1))


def bit_matrix(mask):
    return jnp.where(mask, 1.0, 0.0).astype(bf16)


def dot32(a, b):
    return jnp.dot(a, b, preferred_element_type=f32)


def pack_kernel(tokens, slot_limit, place_ref, asked_ref, rows_ref, *refs):
    out_ref, hot_ref = refs[-2:]
    owners, _, block_count = asked_ref.shape
    pair = rows_ref.shape[1]
    wanted = asked_ref[:, 0, :].astype(f32)
    row, lane = iotas((block_count, block_count))
    rank = dot32(wanted.astype(bf16), bit_matrix(row < lane))
    row, lane = iotas((owners * slot_limit, owners))
    slot = jnp.zeros((owners * slot_limit, block_count), f32)
    for j in range(slot_limit):
        level = jnp.where(rank == j, wanted, 0.0).astype(bf16)
        slot += dot32(bit_matrix(row == lane * slot_limit + j), level)
    slot = slot.astype(bf16)
    for size, first, out in ((pair, place_ref[1] * tokens, None), (tokens, 0, hot_ref)):
        row, lane = iotas((block_count, block_count * size))
        start = row * size
        hot = expand(dot32(slot, bit_matrix((lane >= start) & (lane < start + size))), tokens)
        row, lane = iotas(hot.shape)
        same = (row & (tokens - 1)) + first == (lane & (size - 1))
        hot = jnp.where(same, hot, 0.0).astype(bf16)
        if out is None:
            rows = rows_ref[...].reshape(block_count * size, rows_ref.shape[2])
            out_ref[...] = dot32(hot, rows).astype(bf16)
        else:
            out[...] = hot


def owner_kernel(hot_ref, rows_ref, out_ref):
    total = lax.dot_general(
        hot_ref[...], rows_ref[...], (((0,), (0,)), ((), ())), preferred_element_type=f32
    )
    out_ref[...] = total.astype(bf16)


def slot_hot(ids_ref, tokens, lanes):
    ids = expand(jnp.broadcast_to(ids_ref[:, 0:1], (ids_ref.shape[0], lanes)), tokens)
    row, lane = iotas(ids.shape)
    return bit_matrix(ids * tokens + (row & (tokens - 1)) == lane)


def score_kernel(tokens, pick_ref, own_lim, other_lim, own_ref, other_ref, *refs):
    q_refs, g_refs = refs[:XN], refs[XN : 2 * XN]
    p_ref, gw_ref, stat_ref, key_ref, bias_ref = refs[2 * XN :]
    half = key_ref.shape[0] // CORES
    rows = bias_ref.shape[1]
    query_count = own_lim.shape[1]
    heads = rows // query_count
    value_width = g_refs[0].shape[1]
    row, lane = iotas((query_count, rows))
    start = row * heads
    repeat = bit_matrix((lane >= start) & (lane < start + heads))
    hot = slot_hot(pick_ref, tokens, own_ref.shape[0])
    for h, (lim, part_ref) in enumerate(((own_lim, own_ref), (other_lim, other_ref))):
        part = pl.ds(h * half, half)
        key_ref[part, :] = dot32(hot, part_ref[...]).astype(bf16)
        limit = expand(dot32(lim[...].astype(bf16), repeat), tokens)
        token = (iotas(limit.shape)[0] & (tokens - 1)).astype(f32)
        bias_ref[part, :] = jnp.where(token <= limit, 0.0, -jnp.inf)
    for k in range(XN):
        q, g = q_refs[k][...], g_refs[k][...]
        scores = nt_dot(key_ref[...], q) * (score_scale * log2e) + bias_ref[...]
        peak = jnp.max(scores, axis=0, keepdims=True)
        p = jnp.exp2(scores - peak)
        gw = nt_dot(key_ref[:, :value_width], g)
        p_ref[k] = p.astype(bf16)
        gw_ref[k] = gw
        stat_ref[k, 0:1, :] = peak
        stat_ref[k, 1:2, :] = jnp.sum(p, axis=0, keepdims=True)
        stat_ref[k, 2:3, :] = jnp.sum(p * gw, axis=0, keepdims=True)
        stat_ref[k, 3:8, :] = jnp.zeros((5, peak.shape[1]), f32)


def grad_kernel(tokens, order_ref, key_ref, p_ref, gw_ref, *refs):
    stat_refs, q_refs, g_refs = refs[:XN], refs[XN : 2 * XN], refs[2 * XN : 3 * XN]
    own_ref, other_ref, here_ref, right_ref, left_ref, att3_ref, qg1_ref = refs[3 * XN : -4]
    acc_ref, lhs_ref, rhs_ref, keys_t = refs[-4:]
    rows, width = q_refs[0].shape
    value_width = g_refs[0].shape[1]
    half = key_ref.shape[0] // CORES
    att_out = (
        here_ref.at[:value_width],
        left_ref.at[:value_width],
        right_ref.at[:value_width],
        att3_ref,
    )
    qg_out = (
        here_ref.at[value_width:],
        qg1_ref,
        left_ref.at[value_width:],
        right_ref.at[value_width:],
    )
    rhs_ref[rows:, value_width:] = jnp.zeros((rows, width - value_width), bf16)
    keys_t[...] = key_ref[...].T
    for k in (2, 3, 1, 0):
        stats = [stat_refs[j][(k - j) % XN] for j in range(XN)]
        peak = functools.reduce(jnp.maximum, [s[0:1] for s in stats])
        factors = [jnp.exp2(s[0:1] - peak) for s in stats]
        total = sum(s[1:2] * f for s, f in zip(stats, factors))
        inner = sum(s[2:3] * f for s, f in zip(stats, factors)) / total
        factor = factors[0] / total
        weights = p_ref[k].astype(f32) * factor
        ds = (weights * (gw_ref[k] - inner) * score_scale).astype(bf16)
        w = weights.astype(bf16)
        att_out[k][...] = dot32(keys_t[:value_width, :], w).astype(bf16)
        qg_out[k][...] = dot32(keys_t[...], ds).astype(bf16)
        lhs_ref[:, :rows] = ds
        lhs_ref[:, rows:] = w
        rhs_ref[:rows, :] = q_refs[k][...]
        rhs_ref[rows:, :value_width] = g_refs[k][...]
        grad = dot32(lhs_ref[...], rhs_ref[...])
        if k == 2:
            acc_ref[...] = grad
        else:
            acc_ref[...] += grad
    hot = slot_hot(order_ref, tokens, half)
    own_ref[...] = dot32(hot, acc_ref[:half, :].astype(bf16)).astype(bf16)
    other_ref[...] = dot32(hot, acc_ref[half:, :].astype(bf16)).astype(bf16)


def combine_kernel(here, right, left, att, qg, att_ref, qg_ref):
    value_width = att_ref.shape[1]
    total = here[:value_width].astype(f32) + left[:value_width].astype(f32) + att[...].astype(f32)
    att_ref[...] = total.astype(bf16).T
    total = here[value_width:].astype(f32) + right[value_width:].astype(f32) + qg[...].astype(f32)
    qg_ref[...] = total.astype(bf16).T


def shaped(shape, dtype=bf16):
    return jax.ShapeDtypeStruct(shape, dtype)


def call(kernel, out_shape, operands, name, unused=(), scratch=()):
    return pl.pallas_call(
        kernel,
        out_shape=out_shape,
        in_specs=[pl.BlockSpec(memory_space=pltpu.VMEM)] * len(operands)
        + [pl.BlockSpec(memory_space=pl.ANY)] * len(unused),
        scratch_shapes=list(scratch),
        compiler_params=pltpu.CompilerParams(vmem_limit_bytes=VMEM_LIMIT),
        name=name,
    )(*operands, *unused)


def slot_table(wanted, slot_limit):
    rank_within = jnp.cumsum(wanted.astype(jnp.int32), axis=1) - 1
    local_ids = jnp.arange(wanted.shape[1], dtype=jnp.int32)
    slot_range = jnp.arange(slot_limit, dtype=jnp.int32)
    matches = wanted[:, None, :] & (rank_within[:, None, :] == slot_range[None, :, None])
    present = jnp.any(matches, axis=2)
    found_ids = jnp.sum(jnp.where(matches, local_ids[None, None, :], 0), axis=2)
    return jnp.where(present, found_ids, -1).reshape(-1)


def on_device(queries, latent_cache, output_gradient, selected, positions):
    query_count, head_count, width = queries.shape
    block_count, block_size, _ = latent_cache.shape
    value_width = output_gradient.shape[2]
    owners = lax.axis_size("ctx")
    tp = lax.axis_index("tp")
    tokens = block_size // (XN * CORES)
    slot_limit = (USED - 2) // (owners - 1) + 1
    slots = owners * slot_limit
    rows = query_count * head_count
    half = USED * tokens
    keys = CORES * half
    held = block_count * tokens
    parcels = (owners, slot_limit * tokens, width)

    block_range = jnp.arange(owners * block_count, dtype=jnp.int32)
    wanted = jnp.any(selected.reshape(-1)[:, None] == block_range[None, :], axis=0)
    wanted = wanted.reshape(owners, block_count)
    asked = lax.all_to_all(
        wanted.astype(jnp.int32)[:, None, :], "ctx", split_axis=0, concat_axis=0, tiled=True
    )

    query_rows = queries.reshape(rows, width)
    grad_rows = output_gradient.reshape(rows, value_width)
    q1, q3 = send_x(query_rows, 1), send_x(query_rows, -1)
    g1, g3 = send_x(grad_rows, 1), send_x(grad_rows, -1)
    q2, g2 = send_x(q1, 1), send_x(g3, -1)
    q_parts, g_parts = [query_rows, q1, q2, q3], [grad_rows, g1, g2, g3]

    requests = slot_table(wanted, slot_limit)
    used_slot = requests >= 0
    slot_order = jnp.where(used_slot, jnp.cumsum(used_slot.astype(jnp.int32)) - 1, -1)
    compact = jnp.arange(USED, dtype=jnp.int32)
    slot_match = slot_order[None, :] == compact[:, None]
    slot_ids = jnp.arange(slots, dtype=jnp.int32)
    slot_block = slot_ids // slot_limit * block_count + requests
    picked = jnp.sum(jnp.where(slot_match, slot_ids[None, :], 0), axis=1)
    block_ids = jnp.sum(jnp.where(slot_match, slot_block[None, :], 0), axis=1)
    chosen = jnp.any(selected[None, :, :] == block_ids[:, None, None], axis=2)
    limit = jnp.where(chosen, positions[None, :] - block_ids[:, None] * block_size, -1)
    limit = jnp.clip(limit, -1, block_size - 1)
    own_limit = (limit - tp * tokens).astype(f32)
    other_limit = (limit - (tp ^ 1) * tokens).astype(f32)
    pick = jnp.broadcast_to(picked[:, None], (USED, 128))
    order = jnp.broadcast_to(slot_order[:, None], (slots, 128))

    early = (q1, q2, q3, g1, g2, g3, own_limit, other_limit, pick, order)
    place = jnp.stack([tp // CORES, tp % CORES]).astype(jnp.int32)
    packed, asked_hot = pl.pallas_call(
        functools.partial(pack_kernel, tokens, slot_limit),
        grid_spec=pltpu.PrefetchScalarGridSpec(
            num_scalar_prefetch=1,
            grid=(1,),
            in_specs=[
                pl.BlockSpec((owners, 1, block_count), lambda i, place: (0, 0, 0)),
                pl.BlockSpec(
                    (block_count, CORES * tokens, width), lambda i, place: (0, place[0], 0)
                ),
            ]
            + [pl.BlockSpec(memory_space=pl.ANY)] * len(early),
            out_specs=[
                pl.BlockSpec((slots * tokens, width), lambda i, place: (0, 0)),
                pl.BlockSpec((slots * tokens, held), lambda i, place: (0, 0)),
            ],
        ),
        out_shape=[shaped((slots * tokens, width)), shaped((slots * tokens, held))],
        compiler_params=pltpu.CompilerParams(vmem_limit_bytes=VMEM_LIMIT),
        name="pack",
    )(place, asked, latent_cache, *early)
    fetched = lax.all_to_all(packed.reshape(parcels), "ctx", 0, 0, tiled=True)
    fetched_other = lax.ppermute(fetched, "tp", CORE_SWAP)

    p, gw, stats, key_rows = call(
        functools.partial(score_kernel, tokens),
        [
            shaped((XN, keys, rows)),
            shaped((XN, keys, rows), f32),
            shaped((XN, 8, rows), f32),
            shaped((keys, width)),
        ],
        [
            pick,
            own_limit,
            other_limit,
            fetched.reshape(slots * tokens, width),
            fetched_other.reshape(slots * tokens, width),
            *q_parts,
            *g_parts,
        ],
        "scores",
        scratch=[pltpu.VMEM((keys, rows), f32)],
    )
    all_stats = [stats] + [send_x(stats, k) for k in range(1, XN)]

    both = width + value_width
    own_grad, other_grad, here, right, left, att3, qg1 = call(
        functools.partial(grad_kernel, tokens),
        [shaped((slots * tokens, width))] * 2
        + [shaped((n, rows)) for n in (both, both, both, value_width, width)],
        [order, key_rows, p, gw, *all_stats, *q_parts, *g_parts],
        "grads",
        scratch=[
            pltpu.VMEM((keys, width), f32),
            pltpu.VMEM((keys, 2 * rows), bf16),
            pltpu.VMEM((2 * rows, width), bf16),
            pltpu.VMEM((width, keys), bf16),
        ],
    )
    from_core = lax.ppermute(other_grad.reshape(parcels), "tp", CORE_SWAP)
    returning = (own_grad.reshape(parcels).astype(f32) + from_core.astype(f32)).astype(bf16)
    returned = lax.all_to_all(returning, "ctx", 0, 0, tiled=True)

    right, left = send_x(right, 1), send_x(left, -1)
    att = (att3.astype(f32) + right[:value_width].astype(f32)).astype(bf16)
    qg = (qg1.astype(f32) + left[value_width:].astype(f32)).astype(bf16)
    attended, query_grad = call(
        combine_kernel,
        [shaped((rows, value_width)), shaped((rows, width))],
        [here, right, left, send_x(att, 1), send_x(qg, -1)],
        "combine",
    )
    cache_grad = call(
        owner_kernel,
        shaped((held, width)),
        [asked_hot, returned.reshape(slots * tokens, width)],
        "owner_sum",
    )
    return (
        attended.reshape(query_count, head_count, value_width),
        query_grad.reshape(query_count, head_count, width),
        cache_grad.reshape(block_count, tokens, width),
    )


def solution(mesh):
    in_specs = (
        P("ctx", "tp", None),
        P("ctx", None, None),
        P("ctx", "tp", None),
        P("ctx", None),
        P("ctx"),
    )
    out_specs = (P("ctx", "tp", None), P("ctx", "tp", None), P("ctx", "tp", None))
    return jax.shard_map(
        on_device, mesh=mesh, in_specs=in_specs, out_specs=out_specs, check_vma=False
    )
```

```python
import functools
import math

import jax
import jax.numpy as jnp
from jax import lax
from jax.experimental import pallas as pl
from jax.experimental.pallas import tpu as pltpu
from jax.sharding import PartitionSpec as P

USED = 64
XN = 4
CORES = 2

score_scale = 192.0 ** (-0.5)
log2e = 1.0 / math.log(2.0)
VMEM_LIMIT = 24 * 1024 * 1024
bf16 = jnp.bfloat16
f32 = jnp.float32


def x_shift(k):
    return [
        (x * CORES + c, ((x + k) % XN) * CORES + c) for x in range(XN) for c in range(CORES)
    ]


CORE_SWAP = [(t, t ^ 1) for t in range(XN * CORES)]


def send_x(value, k):
    return lax.ppermute(value, "tp", x_shift(k % XN))


def nt_dot(a, b):
    return lax.dot_general(a, b, (((1,), (1,)), ((), ())), preferred_element_type=f32)


def expand(rows, tokens):
    count, lanes = rows.shape
    wide = jnp.broadcast_to(rows[:, None, :], (count, tokens, lanes))
    return wide.reshape(count * tokens, lanes)


def iotas(shape):
    return (lax.broadcasted_iota(jnp.int32, shape, 0), lax.broadcasted_iota(jnp.int32, shape, 1))


def bit_matrix(mask):
    return jnp.where(mask, 1.0, 0.0).astype(bf16)


def dot32(a, b):
    return jnp.dot(a, b, preferred_element_type=f32)


def pack_kernel(tokens, slot_limit, asked_ref, cache_ref, q_ref, g_ref, *refs):
    out_ref, hot_out, q_out, g_out, rows_ref, hot_ref, sems = refs[-7:]
    owners, _, block_count = asked_ref.shape
    pair = CORES * tokens
    tp = lax.axis_index("tp")
    first = pl.multiple_of(tp // CORES * pair, pair)
    copies = [
        pltpu.make_async_copy(cache_ref.at[:, pl.ds(first, pair), :], rows_ref, sems.at[0]),
        pltpu.make_async_copy(q_ref, q_out, sems.at[1]),
        pltpu.make_async_copy(g_ref, g_out, sems.at[2]),
    ]
    for copy in copies:
        copy.start()
    wanted = asked_ref[:, 0, :].astype(f32)
    row, lane = iotas((block_count, block_count))
    rank = dot32(wanted.astype(bf16), bit_matrix(row < lane))
    row, lane = iotas((owners * slot_limit, owners))
    slot = jnp.zeros((owners * slot_limit, block_count), f32)
    for j in range(slot_limit):
        level = jnp.where(rank == j, wanted, 0.0).astype(bf16)
        slot += dot32(bit_matrix(row == lane * slot_limit + j), level)
    slot = slot.astype(bf16)

    def hot_matrix(size, offset):
        row, lane = iotas((block_count, block_count * size))
        start = row * size
        hot = expand(dot32(slot, bit_matrix((lane >= start) & (lane < start + size))), tokens)
        row, lane = iotas(hot.shape)
        same = (row & (tokens - 1)) + offset == (lane & (size - 1))
        return jnp.where(same, hot, 0.0).astype(bf16)

    hot_ref[...] = hot_matrix(tokens, 0)
    copies.append(pltpu.make_async_copy(hot_ref, hot_out, sems.at[3]))
    copies[3].start()
    hot = hot_matrix(pair, tp % CORES * tokens)
    copies[0].wait()
    rows = rows_ref[...].reshape(block_count * pair, rows_ref.shape[2])
    out_ref[...] = dot32(hot, rows).astype(bf16)
    for copy in copies[1:]:
        copy.wait()


def owner_kernel(hot_ref, rows_ref, out_ref):
    total = lax.dot_general(
        hot_ref[...], rows_ref[...], (((0,), (0,)), ((), ())), preferred_element_type=f32
    )
    out_ref[...] = total.astype(bf16)


def slot_hot(ids_ref, tokens, lanes):
    ids = expand(jnp.broadcast_to(ids_ref[:, 0:1], (ids_ref.shape[0], lanes)), tokens)
    row, lane = iotas(ids.shape)
    return bit_matrix(ids * tokens + (row & (tokens - 1)) == lane)


def unpack_kernel(tokens, pick_ref, rows_ref, *refs):
    hot = slot_hot(pick_ref, tokens, rows_ref.shape[0])
    refs[-1][...] = dot32(hot, rows_ref[...]).astype(bf16)


def score_half(tokens, lim_ref, key_ref, q_refs, g_refs, p_ref, gw_ref):
    rows = p_ref.shape[2]
    query_count = lim_ref.shape[1]
    heads = rows // query_count
    value_width = g_refs[0].shape[1]
    row, lane = iotas((query_count, rows))
    start = row * heads
    repeat = bit_matrix((lane >= start) & (lane < start + heads))
    limit = expand(dot32(lim_ref[...].astype(bf16), repeat), tokens)
    token = (iotas(limit.shape)[0] & (tokens - 1)).astype(f32)
    bias = jnp.where(token <= limit, 0.0, -jnp.inf)
    for k in range(XN):
        scores = nt_dot(key_ref[...], q_refs[k][...]) * (score_scale * log2e) + bias
        peak = jnp.max(scores, axis=0, keepdims=True)
        p = jnp.exp2(scores - peak)
        gw = nt_dot(key_ref[:, :value_width], g_refs[k][...])
        p_ref[k] = p.astype(bf16)
        gw_ref[k] = gw
        total = jnp.sum(p, axis=0, keepdims=True)
        yield k, peak, total, jnp.sum(p * gw, axis=0, keepdims=True)


def own_score_kernel(tokens, lim_ref, key_ref, *refs):
    q_refs, g_refs = refs[:XN], refs[XN : 2 * XN]
    p_ref, gw_ref, stat_ref = refs[2 * XN :]
    for k, peak, total, inner in score_half(
        tokens, lim_ref, key_ref, q_refs, g_refs, p_ref, gw_ref
    ):
        pad = jnp.zeros((5, peak.shape[1]), f32)
        stat_ref[k] = jnp.concatenate([peak, total, inner, pad])


def other_score_kernel(tokens, lim_ref, key_ref, *refs):
    q_refs, g_refs, own_ref = refs[:XN], refs[XN : 2 * XN], refs[2 * XN]
    p_ref, gw_ref, stat_ref = refs[2 * XN + 1 :]
    for k, peak, total, inner in score_half(
        tokens, lim_ref, key_ref, q_refs, g_refs, p_ref, gw_ref
    ):
        own = own_ref[k]
        top = jnp.maximum(peak, own[0:1])
        f_own, f_other = jnp.exp2(own[0:1] - top), jnp.exp2(peak - top)
        total = own[1:2] * f_own + total * f_other
        inner = own[2:3] * f_own + inner * f_other
        pad = jnp.zeros((3, peak.shape[1]), f32)
        stat_ref[k] = jnp.concatenate([top, total, inner, f_own, f_other, pad])


def local_kernel(*refs):
    key_refs, p_refs, gw_refs = refs[:CORES], refs[CORES : 2 * CORES], refs[2 * CORES : 3 * CORES]
    stat_ref, value_ref, grad_ref = refs[3 * CORES :]
    keys_t = [key_ref[...].T for key_ref in key_refs]
    for k in range(XN):
        stats = stat_ref[k]
        inner = stats[2:3] / stats[1:2]
        value, grad = [], []
        for h in range(CORES):
            p = p_refs[h][k].astype(f32) * stats[3 + h : 4 + h]
            value.append(dot32(keys_t[h], p.astype(bf16)))
            grad.append(dot32(keys_t[h], (p * (gw_refs[h][k] - inner)).astype(bf16)))
        value_ref[k] = value[0] + value[1]
        grad_ref[k] = grad[0] + grad[1]


def row_stats(stat_refs, k):
    stats = [stat_refs[j][(k - j) % XN] for j in range(XN)]
    peak = functools.reduce(jnp.maximum, [s[0:1] for s in stats])
    factors = [jnp.exp2(s[0:1] - peak) for s in stats]
    total = sum(s[1:2] * f for s, f in zip(stats, factors))
    inner = sum(s[2:3] * f for s, f in zip(stats, factors)) / total
    return stats[0], inner, factors[0] / total


def key_grad_kernel(tokens, half, order_ref, p_ref, gw_ref, *refs):
    stat_refs, q_refs, g_refs = refs[:XN], refs[XN : 2 * XN], refs[2 * XN : 3 * XN]
    out_ref, sum_ref = refs[-2:]
    value_width = g_refs[0].shape[1]
    key_grad, value_grad = [], []
    for k in range(XN):
        mine, inner, factor = row_stats(stat_refs, k)
        weights = p_ref[k].astype(f32) * (factor * mine[3 + half : 4 + half])
        ds = (weights * (gw_ref[k] - inner) * score_scale).astype(bf16)
        key_grad.append(dot32(ds, q_refs[k][...]))
        value_grad.append(dot32(weights.astype(bf16), g_refs[k][...]))
    key_grad, value_grad = sum(key_grad), sum(value_grad)
    sum_ref[:, :value_width] = (key_grad[:, :value_width] + value_grad).astype(bf16)
    sum_ref[:, value_width:] = key_grad[:, value_width:].astype(bf16)
    hot = slot_hot(order_ref, tokens, sum_ref.shape[0])
    out_ref[...] = dot32(hot, sum_ref[...]).astype(bf16)


def own_grad_kernel(tokens, *refs):
    value_ref, grad_ref = refs[:2]
    stat_refs = refs[5 : 5 + XN]
    outs, sum_ref, sems = refs[-12:-7], refs[-7], refs[-1]
    here_ref, right_ref, left_ref, att3_ref, qg1_ref = refs[-6:-1]
    value_width = att3_ref.shape[0]
    att_out = (
        here_ref.at[:value_width],
        left_ref.at[:value_width],
        right_ref.at[:value_width],
        att3_ref,
    )
    qg_out = (
        here_ref.at[value_width:],
        qg1_ref,
        left_ref.at[value_width:],
        right_ref.at[value_width:],
    )
    for k in range(XN):
        mine, inner, factor = row_stats(stat_refs, k)
        shift = mine[2:3] / mine[1:2] - inner
        att_out[k][...] = (value_ref[k, :value_width] * factor).astype(bf16)
        qg = (grad_ref[k] + value_ref[k] * shift) * (factor * score_scale)
        qg_out[k][...] = qg.astype(bf16)
    copies = [
        pltpu.make_async_copy(src, dst, sems.at[i])
        for i, (src, dst) in enumerate(zip(refs[-6:-1], outs))
    ]
    for copy in copies:
        copy.start()
    key_grad_kernel(tokens, 0, *refs[2:-12], sum_ref)
    for copy in copies:
        copy.wait()


def combine_kernel(here, right, left, att, qg, att_ref, qg_ref):
    value_width = att_ref.shape[1]
    total = here[:value_width].astype(f32) + left[:value_width].astype(f32) + att[...].astype(f32)
    att_ref[...] = total.astype(bf16).T
    total = here[value_width:].astype(f32) + right[value_width:].astype(f32) + qg[...].astype(f32)
    qg_ref[...] = total.astype(bf16).T


def shaped(shape, dtype=bf16):
    return jax.ShapeDtypeStruct(shape, dtype)


def call(kernel, out_shape, operands, name, unused=(), scratch=(), far_in=0, far_out=()):
    vmem, hbm = (pl.BlockSpec(memory_space=m) for m in (pltpu.VMEM, pltpu.HBM))
    near = len(operands) - far_in
    operands = operands[:near] + [
        pltpu.with_memory_space_constraint(x, pltpu.HBM) for x in operands[near:]
    ]
    return pl.pallas_call(
        kernel,
        out_shape=[
            pltpu.HBM(x.shape, x.dtype) if i in far_out else x for i, x in enumerate(out_shape)
        ],
        in_specs=[vmem] * near
        + [hbm] * far_in
        + [pl.BlockSpec(memory_space=pl.ANY)] * len(unused),
        out_specs=[hbm if i in far_out else vmem for i in range(len(out_shape))],
        scratch_shapes=list(scratch),
        compiler_params=pltpu.CompilerParams(vmem_limit_bytes=VMEM_LIMIT),
        name=name,
    )(*operands, *unused)


def slot_table(wanted, slot_limit):
    rank_within = jnp.cumsum(wanted.astype(jnp.int32), axis=1) - 1
    local_ids = jnp.arange(wanted.shape[1], dtype=jnp.int32)
    slot_range = jnp.arange(slot_limit, dtype=jnp.int32)
    matches = wanted[:, None, :] & (rank_within[:, None, :] == slot_range[None, :, None])
    present = jnp.any(matches, axis=2)
    found_ids = jnp.sum(jnp.where(matches, local_ids[None, None, :], 0), axis=2)
    return jnp.where(present, found_ids, -1).reshape(-1)


def on_device(queries, latent_cache, output_gradient, selected, positions):
    query_count, head_count, width = queries.shape
    block_count, block_size, _ = latent_cache.shape
    value_width = output_gradient.shape[2]
    owners = lax.axis_size("ctx")
    tp = lax.axis_index("tp")
    tokens = block_size // (XN * CORES)
    slot_limit = (USED - 2) // (owners - 1) + 1
    slots = owners * slot_limit
    rows = query_count * head_count
    half = USED * tokens
    keys = CORES * half
    held = block_count * tokens
    parcels = (owners, slot_limit * tokens, width)

    block_range = jnp.arange(owners * block_count, dtype=jnp.int32)
    wanted = jnp.any(selected.reshape(-1)[:, None] == block_range[None, :], axis=0)
    wanted = wanted.reshape(owners, block_count)
    asked = lax.all_to_all(
        wanted.astype(jnp.int32)[:, None, :], "ctx", split_axis=0, concat_axis=0, tiled=True
    )

    query_rows = queries.reshape(rows, width)
    grad_rows = output_gradient.reshape(rows, value_width)
    requests = slot_table(wanted, slot_limit)
    used_slot = requests >= 0
    slot_order = jnp.where(used_slot, jnp.cumsum(used_slot.astype(jnp.int32)) - 1, -1)
    compact = jnp.arange(USED, dtype=jnp.int32)
    slot_match = slot_order[None, :] == compact[:, None]
    slot_ids = jnp.arange(slots, dtype=jnp.int32)
    slot_block = slot_ids // slot_limit * block_count + requests
    picked = jnp.sum(jnp.where(slot_match, slot_ids[None, :], 0), axis=1)
    block_ids = jnp.sum(jnp.where(slot_match, slot_block[None, :], 0), axis=1)
    chosen = jnp.any(selected[None, :, :] == block_ids[:, None, None], axis=2)
    limit = jnp.where(chosen, positions[None, :] - block_ids[:, None] * block_size, -1)
    limit = jnp.clip(limit, -1, block_size - 1)
    own_limit = (limit - tp * tokens).astype(f32)
    other_limit = (limit - (tp ^ 1) * tokens).astype(f32)
    pick = jnp.broadcast_to(picked[:, None], (USED, 128))
    order = jnp.broadcast_to(slot_order[:, None], (slots, 128))

    early = (own_limit, other_limit, pick, order)
    packed, asked_hot, q0, g0 = call(
        functools.partial(pack_kernel, tokens, slot_limit),
        [
            shaped((slots * tokens, width)),
            shaped((slots * tokens, held)),
            shaped((rows, width)),
            shaped((rows, value_width)),
        ],
        [asked, latent_cache, query_rows, grad_rows],
        "pack",
        unused=early,
        scratch=[
            pltpu.VMEM((block_count, CORES * tokens, width), bf16),
            pltpu.VMEM((slots * tokens, held), bf16),
            pltpu.SemaphoreType.DMA((4,)),
        ],
        far_in=3,
        far_out=(1,),
    )
    fetched = lax.all_to_all(packed.reshape(parcels), "ctx", 0, 0, tiled=True)

    q1, q3 = send_x(q0, 1), send_x(q0, -1)
    g1, g3 = send_x(g0, 1), send_x(g0, -1)
    q2, g2 = send_x(q1, 1), send_x(g3, -1)
    gathered = [q0, q1, q2, q3, g0, g1, g2, g3]

    (own_keys,) = call(
        functools.partial(unpack_kernel, tokens),
        [shaped((half, width))],
        [pick, fetched.reshape(slots * tokens, width)],
        "unpack",
        unused=(q1, q2, q3, g1, g2, g3),
    )
    other_keys = lax.ppermute(own_keys.reshape(USED, tokens, width), "tp", CORE_SWAP)
    other_keys = other_keys.reshape(half, width)
    score_shapes = [
        shaped((XN, half, rows)),
        shaped((XN, half, rows), f32),
        shaped((XN, 8, rows), f32),
    ]
    own_p, own_gw, own_stats = call(
        functools.partial(own_score_kernel, tokens),
        score_shapes,
        [own_limit, own_keys, *gathered],
        "own_scores",
    )
    other_p, other_gw, stats = call(
        functools.partial(other_score_kernel, tokens),
        score_shapes,
        [other_limit, other_keys, *gathered, own_stats],
        "other_scores",
    )
    all_stats = [stats] + [send_x(stats, k) for k in range(1, XN)]
    value_part, grad_part = call(
        local_kernel,
        [shaped((XN, width, rows), f32)] * 2,
        [own_keys, other_keys, own_p, other_p, own_gw, other_gw, stats],
        "local",
    )

    both = width + value_width
    sum_scratch = [pltpu.VMEM((half, width), bf16)]
    (other_grad,) = call(
        functools.partial(key_grad_kernel, tokens, 1),
        [shaped((slots * tokens, width))],
        [order, other_p, other_gw, *all_stats, *gathered],
        "other_grads",
        unused=(value_part,),
        scratch=sum_scratch,
    )
    from_core = lax.ppermute(other_grad.reshape(parcels), "tp", CORE_SWAP)
    own_grad, here, right, left, att3, qg1 = call(
        functools.partial(own_grad_kernel, tokens),
        [shaped((slots * tokens, width))]
        + [shaped((n, rows)) for n in (both, both, both, value_width, width)],
        [value_part, grad_part, order, own_p, own_gw, *all_stats, *gathered],
        "own_grads",
        scratch=sum_scratch
        + [pltpu.VMEM((n, rows), bf16) for n in (both, both, both, value_width, width)]
        + [pltpu.SemaphoreType.DMA((5,))],
        far_out=(1, 2, 3, 4, 5),
    )
    returning = (own_grad.reshape(parcels).astype(f32) + from_core.astype(f32)).astype(bf16)
    returned = lax.all_to_all(returning, "ctx", 0, 0, tiled=True)

    right, left = send_x(right, 1), send_x(left, -1)
    att = (att3.astype(f32) + right[:value_width].astype(f32)).astype(bf16)
    qg = (qg1.astype(f32) + left[value_width:].astype(f32)).astype(bf16)
    attended, query_grad = call(
        combine_kernel,
        [shaped((rows, value_width)), shaped((rows, width))],
        [here, right, left, send_x(att, 1), send_x(qg, -1)],
        "combine",
    )
    (cache_grad,) = call(
        owner_kernel,
        [shaped((held, width))],
        [asked_hot, returned.reshape(slots * tokens, width)],
        "owner_sum",
    )
    return (
        attended.reshape(query_count, head_count, value_width),
        query_grad.reshape(query_count, head_count, width),
        cache_grad.reshape(block_count, tokens, width),
    )


def solution(mesh):
    in_specs = (
        P("ctx", "tp", None),
        P("ctx", None, None),
        P("ctx", "tp", None),
        P("ctx", None),
        P("ctx"),
    )
    out_specs = (P("ctx", "tp", None), P("ctx", "tp", None), P("ctx", "tp", None))
    return jax.shard_map(
        on_device, mesh=mesh, in_specs=in_specs, out_specs=out_specs, check_vma=False
    )
```

```python
import functools
import math

import jax
import jax.numpy as jnp
from jax import lax
from jax.experimental import pallas as pl
from jax.experimental.pallas import tpu as pltpu
from jax.sharding import PartitionSpec as P

USED = 64
QUERIES = 16
XN = 4
CORES = 2

score_scale = 192.0 ** (-0.5)
log2e = 1.0 / math.log(2.0)
VMEM_LIMIT = 24 * 1024 * 1024
bf16 = jnp.bfloat16
f32 = jnp.float32


def x_shift(k):
    return [
        (x * CORES + c, ((x + k) % XN) * CORES + c) for x in range(XN) for c in range(CORES)
    ]


CORE_SWAP = [(t, t ^ 1) for t in range(XN * CORES)]


def send_x(value, k):
    return lax.ppermute(value, "tp", x_shift(k % XN))


def nt_dot(a, b):
    return lax.dot_general(a, b, (((1,), (1,)), ((), ())), preferred_element_type=f32)


def expand(rows, tokens):
    count, lanes = rows.shape
    wide = jnp.broadcast_to(rows[:, None, :], (count, tokens, lanes))
    return wide.reshape(count * tokens, lanes)


def iotas(shape):
    return (lax.broadcasted_iota(jnp.int32, shape, 0), lax.broadcasted_iota(jnp.int32, shape, 1))


def bit_matrix(mask):
    return jnp.where(mask, 1.0, 0.0).astype(bf16)


def dot32(a, b):
    return jnp.dot(a, b, preferred_element_type=f32)


def pack_kernel(tokens, slot_limit, asked_ref, cache_ref, q_ref, g_ref, *refs):
    out_ref, hot_out, q_out, g_out, rows_ref, hot_ref, sems = refs[-7:]
    owners, _, block_count = asked_ref.shape
    pair = CORES * tokens
    tp = lax.axis_index("tp")
    first = pl.multiple_of(tp // CORES * pair, pair)
    copies = [
        pltpu.make_async_copy(cache_ref.at[:, pl.ds(first, pair), :], rows_ref, sems.at[0]),
        pltpu.make_async_copy(q_ref, q_out, sems.at[1]),
        pltpu.make_async_copy(g_ref, g_out, sems.at[2]),
    ]
    for copy in copies:
        copy.start()
    wanted = asked_ref[:, 0, :].astype(f32)
    row, lane = iotas((block_count, block_count))
    rank = dot32(wanted.astype(bf16), bit_matrix(row < lane))
    row, lane = iotas((owners * slot_limit, owners))
    slot = jnp.zeros((owners * slot_limit, block_count), f32)
    for j in range(slot_limit):
        level = jnp.where(rank == j, wanted, 0.0).astype(bf16)
        slot += dot32(bit_matrix(row == lane * slot_limit + j), level)
    slot = slot.astype(bf16)

    def hot_matrix(size, offset):
        row, lane = iotas((block_count, block_count * size))
        start = row * size
        hot = expand(dot32(slot, bit_matrix((lane >= start) & (lane < start + size))), tokens)
        row, lane = iotas(hot.shape)
        same = (row & (tokens - 1)) + offset == (lane & (size - 1))
        return jnp.where(same, hot, 0.0).astype(bf16)

    hot_ref[...] = hot_matrix(tokens, 0)
    copies.append(pltpu.make_async_copy(hot_ref, hot_out, sems.at[3]))
    copies[3].start()
    hot = hot_matrix(pair, tp % CORES * tokens)
    copies[0].wait()
    rows = rows_ref[...].reshape(block_count * pair, rows_ref.shape[2])
    out_ref[...] = dot32(hot, rows).astype(bf16)
    for copy in copies[1:]:
        copy.wait()


def owner_kernel(hot_ref, rows_ref, out_ref):
    total = lax.dot_general(
        hot_ref[...], rows_ref[...], (((0,), (0,)), ((), ())), preferred_element_type=f32
    )
    out_ref[...] = total.astype(bf16)


def slot_hot(ids, tokens, lanes):
    ids = expand(jnp.broadcast_to(ids, (ids.shape[0], lanes)), tokens)
    row, lane = iotas(ids.shape)
    return bit_matrix(ids * tokens + (row & (tokens - 1)) == lane)


def unpack_kernel(tokens, plan_ref, rows_ref, *refs):
    hot = slot_hot(plan_ref[:USED, 1:2], tokens, rows_ref.shape[0])
    refs[-1][...] = dot32(hot, rows_ref[...]).astype(bf16)


def score_half(tokens, half, plan_ref, key_ref, q_refs, g_refs, p_ref, gw_ref):
    rows = p_ref.shape[2]
    heads = rows // QUERIES
    value_width = g_refs[0].shape[1]
    row, lane = iotas((plan_ref.shape[1], rows))
    start = (row - 2 - half * QUERIES) * heads
    repeat = bit_matrix((lane >= start) & (lane < start + heads))
    limit = expand(dot32(plan_ref[:USED, :].astype(f32).astype(bf16), repeat), tokens)
    token = (iotas(limit.shape)[0] & (tokens - 1)).astype(f32)
    bias = jnp.where(token <= limit, 0.0, -jnp.inf)
    for k in range(XN):
        scores = nt_dot(key_ref[...], q_refs[k][...]) * (score_scale * log2e) + bias
        peak = jnp.max(scores, axis=0, keepdims=True)
        p = jnp.exp2(scores - peak)
        gw = nt_dot(key_ref[:, :value_width], g_refs[k][...])
        p_ref[k] = p.astype(bf16)
        gw_ref[k] = gw
        total = jnp.sum(p, axis=0, keepdims=True)
        yield k, peak, total, jnp.sum(p * gw, axis=0, keepdims=True)


def own_score_kernel(tokens, plan_ref, key_ref, *refs):
    q_refs, g_refs = refs[:XN], refs[XN : 2 * XN]
    p_ref, gw_ref, stat_ref = refs[2 * XN :]
    for k, peak, total, inner in score_half(
        tokens, 0, plan_ref, key_ref, q_refs, g_refs, p_ref, gw_ref
    ):
        pad = jnp.zeros((5, peak.shape[1]), f32)
        stat_ref[k] = jnp.concatenate([peak, total, inner, pad])


def other_score_kernel(tokens, plan_ref, key_ref, *refs):
    q_refs, g_refs, own_ref = refs[:XN], refs[XN : 2 * XN], refs[2 * XN]
    p_ref, gw_ref, stat_ref = refs[2 * XN + 1 :]
    for k, peak, total, inner in score_half(
        tokens, 1, plan_ref, key_ref, q_refs, g_refs, p_ref, gw_ref
    ):
        own = own_ref[k]
        top = jnp.maximum(peak, own[0:1])
        f_own, f_other = jnp.exp2(own[0:1] - top), jnp.exp2(peak - top)
        total = own[1:2] * f_own + total * f_other
        inner = own[2:3] * f_own + inner * f_other
        pad = jnp.zeros((3, peak.shape[1]), f32)
        stat_ref[k] = jnp.concatenate([top, total, inner, f_own, f_other, pad])


def local_kernel(*refs):
    key_refs, p_refs, gw_refs = refs[:CORES], refs[CORES : 2 * CORES], refs[2 * CORES : 3 * CORES]
    stat_ref, value_ref, grad_out, grad_ref, sems = refs[3 * CORES :]
    copies = [
        pltpu.make_async_copy(grad_ref.at[k], grad_out.at[k], sems.at[k]) for k in range(XN)
    ]
    keys_t = [key_ref[...].T for key_ref in key_refs]
    for k in range(XN):
        stats = stat_ref[k]
        inner = stats[2:3] / stats[1:2]
        value, grad = [], []
        for h in range(CORES):
            p = p_refs[h][k].astype(f32) * stats[3 + h : 4 + h]
            value.append(dot32(keys_t[h], p.astype(bf16)))
            grad.append(dot32(keys_t[h], (p * (gw_refs[h][k] - inner)).astype(bf16)))
        value_ref[k] = (value[0] + value[1]).astype(bf16)
        grad_ref[k] = (grad[0] + grad[1]).astype(bf16)
        copies[k].start()
    for copy in copies:
        copy.wait()


def row_stats(stat_refs, k):
    stats = [stat_refs[j][(k - j) % XN] for j in range(XN)]
    peak = functools.reduce(jnp.maximum, [s[0:1] for s in stats])
    factors = [jnp.exp2(s[0:1] - peak) for s in stats]
    total = sum(s[1:2] * f for s, f in zip(stats, factors))
    inner = sum(s[2:3] * f for s, f in zip(stats, factors)) / total
    return stats[0], inner, factors[0] / total


def key_grad_kernel(tokens, half, *refs):
    p_ref, gw_ref = refs[:2]
    stat_refs, q_refs, g_refs = (refs[2 + i * XN : 2 + (i + 1) * XN] for i in range(3))
    last_ref, sum_ref = refs[2 + 3 * XN], refs[-1]
    value_width = g_refs[0].shape[1]
    key_grad, value_grad = [], []
    for k in range(XN):
        mine, inner, factor = row_stats(stat_refs, k)
        factor = factor * mine[3 + half : 4 + half]
        p = p_ref[k].astype(f32)
        ds = (p * (factor * score_scale) * (gw_ref[k] - inner)).astype(bf16)
        key_grad.append(dot32(ds, q_refs[k][...]))
        value_grad.append(dot32((p * factor).astype(bf16), g_refs[k][...]))
    key_grad, value_grad = sum(key_grad), sum(value_grad)
    sum_ref[:, :value_width] = (key_grad[:, :value_width] + value_grad).astype(bf16)
    sum_ref[:, value_width:] = key_grad[:, value_width:].astype(bf16)
    if half == 0:
        hot_ref, out_ref = last_ref, refs[-2]
    else:
        out_ref, hot_ref = refs[-3:-1]
        hot_ref[...] = slot_hot(last_ref[:, 0:1], tokens, sum_ref.shape[0])
    out_ref[...] = dot32(hot_ref[...], sum_ref[...]).astype(bf16)


def scale_kernel(*refs):
    stat_refs, (value_ref, grad_in), outs = refs[:XN], refs[XN : XN + 2], refs[XN + 2 : -2]
    grad_ref, sems = refs[-2:]
    att_refs, qg_refs = outs[:XN], outs[XN:]
    copies = [pltpu.make_async_copy(grad_in.at[k], grad_ref.at[k], sems.at[k]) for k in range(XN)]
    for copy in copies:
        copy.start()
    for k in range(XN):
        copies[k].wait()
        mine, inner, factor = row_stats(stat_refs, k)
        shift = mine[2:3] / mine[1:2] - inner
        value = value_ref[k].astype(f32)
        att_refs[k][...] = (value[: att_refs[k].shape[0]] * factor).astype(bf16)
        qg = (grad_ref[k].astype(f32) + value * shift) * (factor * score_scale)
        qg_refs[k][...] = qg.astype(bf16)


def combine_kernel(*refs):
    for parts, out_ref in ((refs[:3], refs[6]), (refs[3:6], refs[7])):
        total = sum(part[...].astype(f32) for part in parts)
        out_ref[...] = total.astype(bf16).T


def shaped(shape, dtype=bf16):
    return jax.ShapeDtypeStruct(shape, dtype)


def call(
    kernel, out_shape, operands, name, unused=(), unused_far=(), scratch=(), far_in=0, far_out=()
):
    vmem, hbm = (pl.BlockSpec(memory_space=m) for m in (pltpu.VMEM, pltpu.HBM))
    near = len(operands) - far_in
    operands = operands[:near] + [
        pltpu.with_memory_space_constraint(x, pltpu.HBM) for x in operands[near:]
    ]
    return pl.pallas_call(
        kernel,
        out_shape=[
            pltpu.HBM(x.shape, x.dtype) if i in far_out else x for i, x in enumerate(out_shape)
        ],
        in_specs=[vmem] * near
        + [hbm] * far_in
        + [pl.BlockSpec(memory_space=pl.ANY)] * len(unused)
        + [hbm] * len(unused_far),
        out_specs=[hbm if i in far_out else vmem for i in range(len(out_shape))],
        scratch_shapes=list(scratch),
        compiler_params=pltpu.CompilerParams(vmem_limit_bytes=VMEM_LIMIT),
        name=name,
    )(
        *operands,
        *unused,
        *(pltpu.with_memory_space_constraint(x, pltpu.HBM) for x in unused_far),
    )


def slot_table(wanted, slot_limit):
    rank_within = jnp.cumsum(wanted.astype(jnp.int32), axis=1) - 1
    local_ids = jnp.arange(wanted.shape[1], dtype=jnp.int32)
    slot_range = jnp.arange(slot_limit, dtype=jnp.int32)
    matches = wanted[:, None, :] & (rank_within[:, None, :] == slot_range[None, :, None])
    present = jnp.any(matches, axis=2)
    found_ids = jnp.sum(jnp.where(matches, local_ids[None, None, :], 0), axis=2)
    return jnp.where(present, found_ids, -1).reshape(-1)


def on_device(queries, latent_cache, output_gradient, selected, positions):
    query_count, head_count, width = queries.shape
    block_count, block_size, _ = latent_cache.shape
    value_width = output_gradient.shape[2]
    owners = lax.axis_size("ctx")
    tp = lax.axis_index("tp")
    tokens = block_size // (XN * CORES)
    slot_limit = (USED - 2) // (owners - 1) + 1
    slots = owners * slot_limit
    rows = query_count * head_count
    half = USED * tokens
    keys = CORES * half
    held = block_count * tokens
    parcels = (owners, slot_limit * tokens, width)

    block_range = jnp.arange(owners * block_count, dtype=jnp.int32)
    wanted = jnp.any(selected.reshape(-1)[:, None] == block_range[None, :], axis=0)
    wanted = wanted.reshape(owners, block_count)
    asked = lax.all_to_all(
        wanted.astype(jnp.int32)[:, None, :], "ctx", split_axis=0, concat_axis=0, tiled=True
    )

    query_rows = queries.reshape(rows, width)
    grad_rows = output_gradient.reshape(rows, value_width)
    requests = slot_table(wanted, slot_limit)
    used_slot = requests >= 0
    slot_order = jnp.where(used_slot, jnp.cumsum(used_slot.astype(jnp.int32)) - 1, -1)
    compact = jnp.arange(USED, dtype=jnp.int32)
    slot_match = slot_order[None, :] == compact[:, None]
    slot_ids = jnp.arange(slots, dtype=jnp.int32)
    slot_block = slot_ids // slot_limit * block_count + requests
    picked = jnp.sum(jnp.where(slot_match, slot_ids[None, :], 0), axis=1)
    block_ids = jnp.sum(jnp.where(slot_match, slot_block[None, :], 0), axis=1)
    chosen = jnp.any(selected[None, :, :] == block_ids[:, None, None], axis=2)
    limit = jnp.where(chosen, positions[None, :] - block_ids[:, None] * block_size, -1)
    limit = jnp.clip(limit, -1, block_size - 1)
    columns = [picked[:, None], limit - tp * tokens, limit - (tp ^ 1) * tokens]
    plan = jnp.pad(jnp.concatenate(columns, axis=1), ((0, slots - USED), (0, 0)))
    plan = jnp.concatenate([slot_order[:, None], plan], axis=1)
    plan = jnp.pad(plan, ((0, 0), (0, 128 - plan.shape[1])))

    packed, asked_hot, q0, g0 = call(
        functools.partial(pack_kernel, tokens, slot_limit),
        [
            shaped((slots * tokens, width)),
            shaped((slots * tokens, held)),
            shaped((rows, width)),
            shaped((rows, value_width)),
        ],
        [asked, latent_cache, query_rows, grad_rows],
        "pack",
        unused=(plan,),
        scratch=[
            pltpu.VMEM((block_count, CORES * tokens, width), bf16),
            pltpu.VMEM((slots * tokens, held), bf16),
            pltpu.SemaphoreType.DMA((4,)),
        ],
        far_in=3,
        far_out=(1,),
    )
    fetched = lax.all_to_all(packed.reshape(parcels), "ctx", 0, 0, tiled=True)

    q1, q3 = send_x(q0, 1), send_x(q0, -1)
    g1, g3 = send_x(g0, 1), send_x(g0, -1)
    q2, g2 = send_x(q1, 1), send_x(g3, -1)
    gathered = [q0, q1, q2, q3, g0, g1, g2, g3]

    (own_keys,) = call(
        functools.partial(unpack_kernel, tokens),
        [shaped((half, width))],
        [plan, fetched.reshape(slots * tokens, width)],
        "unpack",
        unused=(q1, q2, q3, g1, g2, g3),
    )
    other_keys = lax.ppermute(own_keys.reshape(USED, tokens, width), "tp", CORE_SWAP)
    other_keys = other_keys.reshape(half, width)
    score_shapes = [
        shaped((XN, half, rows)),
        shaped((XN, half, rows), f32),
        shaped((XN, 8, rows), f32),
    ]
    own_p, own_gw, own_stats = call(
        functools.partial(own_score_kernel, tokens),
        score_shapes,
        [plan, own_keys, *gathered],
        "own_scores",
    )
    other_p, other_gw, stats = call(
        functools.partial(other_score_kernel, tokens),
        score_shapes,
        [plan, other_keys, *gathered, own_stats],
        "other_scores",
    )
    all_stats = [stats] + [send_x(stats, k) for k in range(1, XN)]
    part_shape = (XN, width, rows)
    part_scratch = [pltpu.VMEM(part_shape, bf16), pltpu.SemaphoreType.DMA((XN,))]
    value_part, grad_part = call(
        local_kernel,
        [shaped(part_shape)] * 2,
        [own_keys, other_keys, own_p, other_p, own_gw, other_gw, stats],
        "local",
        far_out=(1,),
        scratch=part_scratch,
    )

    grad_shape = shaped((slots * tokens, width))
    sum_scratch = [pltpu.VMEM((half, width), bf16)]
    other_grad, spread_hot = call(
        functools.partial(key_grad_kernel, tokens, 1),
        [grad_shape, shaped((slots * tokens, half))],
        [other_p, other_gw, *all_stats, *gathered, plan],
        "other_grads",
        unused=(value_part,),
        scratch=sum_scratch,
    )
    from_core = lax.ppermute(other_grad.reshape(parcels), "tp", CORE_SWAP)
    (own_grad,) = call(
        functools.partial(key_grad_kernel, tokens, 0),
        [grad_shape],
        [own_p, own_gw, *all_stats, *gathered, spread_hot],
        "own_grads",
        scratch=sum_scratch,
    )
    returning = (own_grad.reshape(parcels).astype(f32) + from_core.astype(f32)).astype(bf16)
    returned = lax.all_to_all(returning, "ctx", 0, 0, tiled=True)

    out_shapes = [(value_width, rows)] * XN + [(width, rows)] * XN
    outs = call(
        scale_kernel,
        [shaped(x) for x in out_shapes],
        [*all_stats, value_part, grad_part],
        "scale",
        far_in=1,
        scratch=part_scratch,
    )
    att, qg = outs[:XN], outs[XN:]
    att_far, qg_far = send_x(att[2], 1), send_x(qg[2], -1)
    qg_left, att_right = send_x(qg[3], 1), send_x(att[1], -1)
    att_left = (att[3].astype(f32) + att_far.astype(f32)).astype(bf16)
    qg_right = (qg[1].astype(f32) + qg_far.astype(f32)).astype(bf16)
    attended, query_grad = call(
        combine_kernel,
        [shaped((rows, value_width)), shaped((rows, width))],
        [att[0], send_x(att_left, 1), att_right, qg[0], qg_left, send_x(qg_right, -1)],
        "combine",
    )
    (cache_grad,) = call(
        owner_kernel,
        [shaped((held, width))],
        [asked_hot, returned.reshape(slots * tokens, width)],
        "owner_sum",
    )
    return (
        attended.reshape(query_count, head_count, value_width),
        query_grad.reshape(query_count, head_count, width),
        cache_grad.reshape(block_count, tokens, width),
    )


def solution(mesh):
    in_specs = (
        P("ctx", "tp", None),
        P("ctx", None, None),
        P("ctx", "tp", None),
        P("ctx", None),
        P("ctx"),
    )
    out_specs = (P("ctx", "tp", None), P("ctx", "tp", None), P("ctx", "tp", None))
    return jax.shard_map(
        on_device, mesh=mesh, in_specs=in_specs, out_specs=out_specs, check_vma=False
    )
```

```python
import functools
import math

import jax
import jax.numpy as jnp
from jax import lax
from jax.experimental import pallas as pl
from jax.experimental.pallas import tpu as pltpu
from jax.sharding import PartitionSpec as P

USED = 64
QUERIES = 16
XN = 4
CORES = 2

score_scale = 192.0 ** (-0.5)
log2e = 1.0 / math.log(2.0)
VMEM_LIMIT = 24 * 1024 * 1024
bf16 = jnp.bfloat16
f32 = jnp.float32


def x_shift(k):
    return [
        (x * CORES + c, ((x + k) % XN) * CORES + c) for x in range(XN) for c in range(CORES)
    ]


CORE_SWAP = [(t, t ^ 1) for t in range(XN * CORES)]


def send_x(value, k):
    return lax.ppermute(value, "tp", x_shift(k % XN))


def nt_dot(a, b):
    return lax.dot_general(a, b, (((1,), (1,)), ((), ())), preferred_element_type=f32)


def expand(rows, tokens):
    count, lanes = rows.shape
    wide = jnp.broadcast_to(rows[:, None, :], (count, tokens, lanes))
    return wide.reshape(count * tokens, lanes)


def iotas(shape):
    return (lax.broadcasted_iota(jnp.int32, shape, 0), lax.broadcasted_iota(jnp.int32, shape, 1))


def bit_matrix(mask):
    return jnp.where(mask, 1.0, 0.0).astype(bf16)


def dot32(a, b):
    return jnp.dot(a, b, preferred_element_type=f32)


def to_parcels(rows, shape, slot_limit):
    owners, height, lanes = shape
    count = rows.shape[0] // owners
    tokens = count // slot_limit
    full = rows.shape[1] // lanes
    parts = [
        rows[:, c * lanes : (c + 1) * lanes].reshape(owners, count, lanes) for c in range(full)
    ]
    tail = rows[:, full * lanes :].reshape(owners, count, rows.shape[1] - full * lanes)
    tails = [tail[:, j * tokens : (j + 1) * tokens] for j in range(slot_limit)]
    tails += [jnp.zeros_like(tails[0])] * (slot_limit % 2)
    for j in range(0, len(tails), 2):
        parts.append(jnp.concatenate(tails[j : j + 2], axis=2))
    return jnp.concatenate(parts, axis=1).astype(bf16)


def from_parcels(parcel_ref, count, slot_limit):
    owners, height, lanes = parcel_ref.shape
    tokens = count // slot_limit
    parcels = parcel_ref[...].astype(f32)
    full = height // count
    parts = [
        parcels[:, c * count : (c + 1) * count].reshape(owners * count, lanes) for c in range(full)
    ]
    tails = []
    for j in range(slot_limit):
        first = full * count + j // 2 * tokens
        pair = parcels[:, first : first + tokens]
        tails.append(pair[:, :, j % 2 * (lanes // 2) : (j % 2 + 1) * (lanes // 2)])
    parts.append(jnp.concatenate(tails, axis=1).reshape(owners * count, lanes // 2))
    return jnp.concatenate(parts, axis=1).astype(bf16)


def pack_kernel(tokens, slot_limit, asked_ref, cache_ref, q_ref, g_ref, *refs):
    out_ref, hot_out, q_out, g_out, rows_ref, hot_ref, sems = refs[-7:]
    owners, _, block_count = asked_ref.shape
    pair = CORES * tokens
    tp = lax.axis_index("tp")
    first = pl.multiple_of(tp // CORES * pair, pair)
    copies = [
        pltpu.make_async_copy(cache_ref.at[:, pl.ds(first, pair), :], rows_ref, sems.at[0]),
        pltpu.make_async_copy(q_ref, q_out, sems.at[1]),
        pltpu.make_async_copy(g_ref, g_out, sems.at[2]),
    ]
    for copy in copies:
        copy.start()
    wanted = asked_ref[:, 0, :].astype(f32)
    row, lane = iotas((block_count, block_count))
    rank = dot32(wanted.astype(bf16), bit_matrix(row < lane))
    row, lane = iotas((owners * slot_limit, owners))
    slot = jnp.zeros((owners * slot_limit, block_count), f32)
    for j in range(slot_limit):
        level = jnp.where(rank == j, wanted, 0.0).astype(bf16)
        slot += dot32(bit_matrix(row == lane * slot_limit + j), level)
    slot = slot.astype(bf16)

    row, lane = iotas((block_count, block_count * tokens))
    start = row * tokens
    hot = expand(dot32(slot, bit_matrix((lane >= start) & (lane < start + tokens))), tokens)
    row, lane = iotas(hot.shape)
    hot = jnp.where((row & (tokens - 1)) == (lane & (tokens - 1)), hot, 0.0).astype(bf16)
    hot_ref[...] = hot
    copies.append(pltpu.make_async_copy(hot_ref, hot_out, sems.at[3]))
    copies[3].start()
    copies[0].wait()
    rows = rows_ref[...].astype(f32)
    rows = jnp.where(tp % CORES == 0, rows[:, :tokens], rows[:, tokens:])
    rows = rows.reshape(block_count * tokens, rows_ref.shape[2]).astype(bf16)
    out_ref[...] = to_parcels(dot32(hot, rows), out_ref.shape, slot_limit)
    for copy in copies[1:]:
        copy.wait()


def owner_kernel(slot_limit, hot_ref, parcel_ref, out_ref):
    count = hot_ref.shape[0] // parcel_ref.shape[0]
    rows = from_parcels(parcel_ref, count, slot_limit)
    total = lax.dot_general(
        hot_ref[...], rows, (((0,), (0,)), ((), ())), preferred_element_type=f32
    )
    out_ref[...] = total.astype(bf16)


def slot_hot(ids, tokens, lanes):
    ids = expand(jnp.broadcast_to(ids, (ids.shape[0], lanes)), tokens)
    row, lane = iotas(ids.shape)
    return bit_matrix(ids * tokens + (row & (tokens - 1)) == lane)


def unpack_kernel(tokens, slot_limit, plan_ref, parcel_ref, *refs):
    count = slot_limit * tokens
    hot = slot_hot(plan_ref[:USED, 1:2], tokens, parcel_ref.shape[0] * count)
    rows = from_parcels(parcel_ref, count, slot_limit)
    refs[-1][...] = dot32(hot, rows).astype(bf16)


def score_half(tokens, half, plan_ref, key_ref, q_refs, g_refs, p_ref, gw_ref):
    rows = p_ref.shape[2]
    heads = rows // QUERIES
    value_width = g_refs[0].shape[1]
    row, lane = iotas((plan_ref.shape[1], rows))
    start = (row - 2 - half * QUERIES) * heads
    repeat = bit_matrix((lane >= start) & (lane < start + heads))
    limit = expand(dot32(plan_ref[:USED, :].astype(f32).astype(bf16), repeat), tokens)
    token = (iotas(limit.shape)[0] & (tokens - 1)).astype(f32)
    bias = jnp.where(token <= limit, 0.0, -jnp.inf)
    for k in range(XN):
        scores = nt_dot(key_ref[...], q_refs[k][...]) * (score_scale * log2e) + bias
        peak = jnp.max(scores, axis=0, keepdims=True)
        p = jnp.exp2(scores - peak)
        gw = nt_dot(key_ref[:, :value_width], g_refs[k][...])
        p_ref[k] = p.astype(bf16)
        gw_ref[k] = gw
        total = jnp.sum(p, axis=0, keepdims=True)
        yield k, peak, total, jnp.sum(p * gw, axis=0, keepdims=True)


def own_score_kernel(tokens, plan_ref, key_ref, *refs):
    q_refs, g_refs = refs[:XN], refs[XN : 2 * XN]
    p_ref, gw_ref, stat_ref = refs[2 * XN :]
    for k, peak, total, inner in score_half(
        tokens, 0, plan_ref, key_ref, q_refs, g_refs, p_ref, gw_ref
    ):
        pad = jnp.zeros((5, peak.shape[1]), f32)
        stat_ref[k] = jnp.concatenate([peak, total, inner, pad])


def other_score_kernel(tokens, plan_ref, key_ref, *refs):
    q_refs, g_refs, own_ref = refs[:XN], refs[XN : 2 * XN], refs[2 * XN]
    p_ref, gw_ref, stat_ref = refs[2 * XN + 1 :]
    for k, peak, total, inner in score_half(
        tokens, 1, plan_ref, key_ref, q_refs, g_refs, p_ref, gw_ref
    ):
        own = own_ref[k]
        top = jnp.maximum(peak, own[0:1])
        f_own, f_other = jnp.exp2(own[0:1] - top), jnp.exp2(peak - top)
        total = own[1:2] * f_own + total * f_other
        inner = own[2:3] * f_own + inner * f_other
        pad = jnp.zeros((3, peak.shape[1]), f32)
        stat_ref[k] = jnp.concatenate([top, total, inner, f_own, f_other, pad])


def local_kernel(*refs):
    key_refs, p_refs, gw_refs = refs[:CORES], refs[CORES : 2 * CORES], refs[2 * CORES : 3 * CORES]
    stat_ref, value_ref, grad_ref = refs[3 * CORES :]
    keys_t = [key_ref[...].T for key_ref in key_refs]
    for k in range(XN):
        stats = stat_ref[k]
        inner = stats[2:3] / stats[1:2]
        value, grad = [], []
        for h in range(CORES):
            p = p_refs[h][k].astype(f32) * stats[3 + h : 4 + h]
            value.append(dot32(keys_t[h], p.astype(bf16)))
            grad.append(dot32(keys_t[h], (p * (gw_refs[h][k] - inner)).astype(bf16)))
        value_ref[k] = (value[0] + value[1]).astype(bf16)
        grad_ref[k] = (grad[0] + grad[1]).astype(bf16)


def row_stats(stat_refs, k):
    stats = [stat_refs[j][(k - j) % XN] for j in range(XN)]
    peak = functools.reduce(jnp.maximum, [s[0:1] for s in stats])
    factors = [jnp.exp2(s[0:1] - peak) for s in stats]
    total = sum(s[1:2] * f for s, f in zip(stats, factors))
    inner = sum(s[2:3] * f for s, f in zip(stats, factors)) / total
    return stats[0], inner, factors[0] / total


def key_grad_kernel(tokens, slot_limit, half, *refs):
    p_ref, gw_ref = refs[:2]
    stat_refs, q_refs, g_refs = (refs[2 + i * XN : 2 + (i + 1) * XN] for i in range(3))
    last_ref, part_ref = refs[2 + 3 * XN : 4 + 3 * XN]
    if half == 0:
        out_ref, part_out, sum_ref, sem = refs[-4:]
    else:
        out_ref, part_out, hot_ref, sum_ref, sem = refs[-5:]
    copy = pltpu.make_async_copy(part_ref, part_out, sem)
    copy.start()
    value_width = g_refs[0].shape[1]
    key_grad, value_grad = [], []
    for k in range(XN):
        mine, inner, factor = row_stats(stat_refs, k)
        factor = factor * mine[3 + half : 4 + half]
        p = p_ref[k].astype(f32)
        ds = (p * (factor * score_scale) * (gw_ref[k] - inner)).astype(bf16)
        key_grad.append(dot32(ds, q_refs[k][...]))
        value_grad.append(dot32((p * factor).astype(bf16), g_refs[k][...]))
    key_grad, value_grad = sum(key_grad), sum(value_grad)
    sum_ref[:, :value_width] = (key_grad[:, :value_width] + value_grad).astype(bf16)
    sum_ref[:, value_width:] = key_grad[:, value_width:].astype(bf16)
    if half == 0:
        hot_ref = last_ref
    else:
        hot_ref[...] = slot_hot(last_ref[:, 0:1], tokens, sum_ref.shape[0])
    rows = dot32(hot_ref[...], sum_ref[...])
    out_ref[...] = to_parcels(rows, out_ref.shape, slot_limit)
    copy.wait()


def scale_kernel(blocks, *refs):
    stat_refs, ins, outs = refs[:XN], refs[XN : XN + 2], refs[XN + 2 : -3]
    value_ref, grad_ref, sems = refs[-3:]
    copies = {
        (k, i): pltpu.make_async_copy(src.at[k], dst.at[k], sems.at[k, i])
        for k in blocks
        for i, (src, dst) in enumerate(zip(ins, (value_ref, grad_ref)))
    }
    for copy in copies.values():
        copy.start()
    for att_ref, qg_ref, k in zip(outs[::2], outs[1::2], blocks):
        copies[k, 0].wait()
        copies[k, 1].wait()
        mine, inner, factor = row_stats(stat_refs, k)
        shift = mine[2:3] / mine[1:2] - inner
        value = value_ref[k].astype(f32)
        att_ref[...] = (value[: att_ref.shape[0]] * factor).astype(bf16)
        qg = (grad_ref[k].astype(f32) + value * shift) * (factor * score_scale)
        qg_ref[...] = qg.astype(bf16)


def combine_kernel(*refs):
    for parts, out_ref in ((refs[:3], refs[6]), (refs[3:6], refs[7])):
        total = sum(part[...].astype(f32) for part in parts)
        out_ref[...] = total.astype(bf16).T


def shaped(shape, dtype=bf16):
    return jax.ShapeDtypeStruct(shape, dtype)


def call(
    kernel, out_shape, operands, name, unused=(), unused_far=(), scratch=(), far_in=0, far_out=()
):
    vmem, hbm = (pl.BlockSpec(memory_space=m) for m in (pltpu.VMEM, pltpu.HBM))
    near = len(operands) - far_in
    operands = operands[:near] + [
        pltpu.with_memory_space_constraint(x, pltpu.HBM) for x in operands[near:]
    ]
    return pl.pallas_call(
        kernel,
        out_shape=[
            pltpu.HBM(x.shape, x.dtype) if i in far_out else x for i, x in enumerate(out_shape)
        ],
        in_specs=[vmem] * near
        + [hbm] * far_in
        + [pl.BlockSpec(memory_space=pl.ANY)] * len(unused)
        + [hbm] * len(unused_far),
        out_specs=[hbm if i in far_out else vmem for i in range(len(out_shape))],
        scratch_shapes=list(scratch),
        compiler_params=pltpu.CompilerParams(vmem_limit_bytes=VMEM_LIMIT),
        name=name,
    )(
        *operands,
        *unused,
        *(pltpu.with_memory_space_constraint(x, pltpu.HBM) for x in unused_far),
    )


def slot_table(wanted, slot_limit):
    rank_within = jnp.cumsum(wanted.astype(jnp.int32), axis=1) - 1
    local_ids = jnp.arange(wanted.shape[1], dtype=jnp.int32)
    slot_range = jnp.arange(slot_limit, dtype=jnp.int32)
    matches = wanted[:, None, :] & (rank_within[:, None, :] == slot_range[None, :, None])
    present = jnp.any(matches, axis=2)
    found_ids = jnp.sum(jnp.where(matches, local_ids[None, None, :], 0), axis=2)
    return jnp.where(present, found_ids, -1).reshape(-1)


def on_device(queries, latent_cache, output_gradient, selected, positions):
    query_count, head_count, width = queries.shape
    block_count, block_size, _ = latent_cache.shape
    value_width = output_gradient.shape[2]
    owners = lax.axis_size("ctx")
    tp = lax.axis_index("tp")
    tokens = block_size // (XN * CORES)
    slot_limit = (USED - 2) // (owners - 1) + 1
    slots = owners * slot_limit
    rows = query_count * head_count
    half = USED * tokens
    keys = CORES * half
    held = block_count * tokens
    whole, tail = divmod(width, 128)
    height = (whole * slot_limit + -(-slot_limit * tail // 128)) * tokens
    parcels = (owners, height, 128)

    block_range = jnp.arange(owners * block_count, dtype=jnp.int32)
    wanted = jnp.any(selected.reshape(-1)[:, None] == block_range[None, :], axis=0)
    wanted = wanted.reshape(owners, block_count)
    asked = lax.all_to_all(
        wanted.astype(jnp.int32)[:, None, :], "ctx", split_axis=0, concat_axis=0, tiled=True
    )

    query_rows = queries.reshape(rows, width)
    grad_rows = output_gradient.reshape(rows, value_width)
    requests = slot_table(wanted, slot_limit)
    used_slot = requests >= 0
    slot_order = jnp.where(used_slot, jnp.cumsum(used_slot.astype(jnp.int32)) - 1, -1)
    compact = jnp.arange(USED, dtype=jnp.int32)
    slot_match = slot_order[None, :] == compact[:, None]
    slot_ids = jnp.arange(slots, dtype=jnp.int32)
    slot_block = slot_ids // slot_limit * block_count + requests
    picked = jnp.sum(jnp.where(slot_match, slot_ids[None, :], 0), axis=1)
    block_ids = jnp.sum(jnp.where(slot_match, slot_block[None, :], 0), axis=1)
    chosen = jnp.any(selected[None, :, :] == block_ids[:, None, None], axis=2)
    limit = jnp.where(chosen, positions[None, :] - block_ids[:, None] * block_size, -1)
    limit = jnp.clip(limit, -1, block_size - 1)
    columns = [picked[:, None], limit - tp * tokens, limit - (tp ^ 1) * tokens]
    plan = jnp.pad(jnp.concatenate(columns, axis=1), ((0, slots - USED), (0, 0)))
    plan = jnp.concatenate([slot_order[:, None], plan], axis=1)
    plan = jnp.pad(plan, ((0, 0), (0, 128 - plan.shape[1])))

    packed, asked_hot, q0, g0 = call(
        functools.partial(pack_kernel, tokens, slot_limit),
        [
            shaped(parcels),
            shaped((slots * tokens, held)),
            shaped((rows, width)),
            shaped((rows, value_width)),
        ],
        [asked, latent_cache, query_rows, grad_rows],
        "pack",
        unused=(plan,),
        scratch=[
            pltpu.VMEM((block_count, CORES * tokens, width), bf16),
            pltpu.VMEM((slots * tokens, held), bf16),
            pltpu.SemaphoreType.DMA((4,)),
        ],
        far_in=3,
        far_out=(1,),
    )
    fetched = lax.all_to_all(packed, "ctx", 0, 0, tiled=True)

    q1, q3 = send_x(q0, 1), send_x(q0, -1)
    g1, g3 = send_x(g0, 1), send_x(g0, -1)
    q2, g2 = send_x(q1, 1), send_x(g3, -1)
    gathered = [q0, q1, q2, q3, g0, g1, g2, g3]

    (own_keys,) = call(
        functools.partial(unpack_kernel, tokens, slot_limit),
        [shaped((half, width))],
        [plan, fetched],
        "unpack",
        unused=(q1, q2, q3, g1, g2, g3),
    )
    other_keys = lax.ppermute(own_keys.reshape(USED, tokens, width), "tp", CORE_SWAP)
    other_keys = other_keys.reshape(half, width)
    score_shapes = [
        shaped((XN, half, rows)),
        shaped((XN, half, rows), f32),
        shaped((XN, 8, rows), f32),
    ]
    own_p, own_gw, own_stats = call(
        functools.partial(own_score_kernel, tokens),
        score_shapes,
        [plan, own_keys, *gathered],
        "own_scores",
    )
    other_p, other_gw, stats = call(
        functools.partial(other_score_kernel, tokens),
        score_shapes,
        [plan, other_keys, *gathered, own_stats],
        "other_scores",
    )
    all_stats = [stats] + [send_x(stats, k) for k in range(1, XN)]
    part_shape = (XN, width, rows)
    part_scratch = [
        pltpu.VMEM(part_shape, bf16),
        pltpu.VMEM(part_shape, bf16),
        pltpu.SemaphoreType.DMA((XN, 2)),
    ]
    value_part, grad_part = call(
        local_kernel,
        [shaped(part_shape)] * 2,
        [own_keys, other_keys, own_p, other_p, own_gw, other_gw, stats],
        "local",
    )

    grad_shape = shaped(parcels)
    sum_scratch = [pltpu.VMEM((half, width), bf16), pltpu.SemaphoreType.DMA(())]
    other_grad, value_part, spread_hot = call(
        functools.partial(key_grad_kernel, tokens, slot_limit, 1),
        [grad_shape, shaped(part_shape), shaped((slots * tokens, half))],
        [other_p, other_gw, *all_stats, *gathered, plan, value_part],
        "other_grads",
        far_out=(1,),
        scratch=sum_scratch,
    )
    from_core = lax.ppermute(other_grad, "tp", CORE_SWAP)
    own_grad, grad_part = call(
        functools.partial(key_grad_kernel, tokens, slot_limit, 0),
        [grad_shape, shaped(part_shape)],
        [own_p, own_gw, *all_stats, *gathered, spread_hot, grad_part],
        "own_grads",
        far_out=(1,),
        scratch=sum_scratch,
    )
    returning = (own_grad.astype(f32) + from_core.astype(f32)).astype(bf16)
    returned = lax.all_to_all(returning, "ctx", 0, 0, tiled=True)

    att, qg = {}, {}
    for blocks in ((2,), (3, 1, 0)):
        outs = call(
            functools.partial(scale_kernel, blocks),
            [shaped((value_width, rows)), shaped((width, rows))] * len(blocks),
            [*all_stats, value_part, grad_part],
            "scale",
            far_in=2,
            scratch=part_scratch,
        )
        att.update(zip(blocks, outs[::2]))
        qg.update(zip(blocks, outs[1::2]))
    att_far, qg_far = send_x(att[2], 1), send_x(qg[2], -1)
    qg_left, att_right = send_x(qg[3], 1), send_x(att[1], -1)
    att_left = (att[3].astype(f32) + att_far.astype(f32)).astype(bf16)
    qg_right = (qg[1].astype(f32) + qg_far.astype(f32)).astype(bf16)
    attended, query_grad = call(
        combine_kernel,
        [shaped((rows, value_width)), shaped((rows, width))],
        [att[0], send_x(att_left, 1), att_right, qg[0], qg_left, send_x(qg_right, -1)],
        "combine",
    )
    (cache_grad,) = call(
        functools.partial(owner_kernel, slot_limit),
        [shaped((held, width))],
        [asked_hot, returned],
        "owner_sum",
    )
    return (
        attended.reshape(query_count, head_count, value_width),
        query_grad.reshape(query_count, head_count, width),
        cache_grad.reshape(block_count, tokens, width),
    )


def solution(mesh):
    in_specs = (
        P("ctx", "tp", None),
        P("ctx", None, None),
        P("ctx", "tp", None),
        P("ctx", None),
        P("ctx"),
    )
    out_specs = (P("ctx", "tp", None), P("ctx", "tp", None), P("ctx", "tp", None))
    return jax.shard_map(
        on_device, mesh=mesh, in_specs=in_specs, out_specs=out_specs, check_vma=False
    )
```

```python
import functools
import math

import jax
import jax.numpy as jnp
from jax import lax
from jax.experimental import pallas as pl
from jax.experimental.pallas import tpu as pltpu
from jax.sharding import PartitionSpec as P

USED = 64
QUERIES = 16
XN = 4
CORES = 2
PARTS = 4

score_scale = 192.0 ** (-0.5)
log2e = 1.0 / math.log(2.0)
VMEM_LIMIT = 24 * 1024 * 1024
bf16 = jnp.bfloat16
f32 = jnp.float32


def x_shift(k):
    return [
        (x * CORES + c, ((x + k) % XN) * CORES + c) for x in range(XN) for c in range(CORES)
    ]


CORE_SWAP = [(t, t ^ 1) for t in range(XN * CORES)]


def send_x(value, k):
    return lax.ppermute(value, "tp", x_shift(k % XN))


def nt_dot(a, b):
    return lax.dot_general(a, b, (((1,), (1,)), ((), ())), preferred_element_type=f32)


def expand(rows, tokens):
    count, lanes = rows.shape
    wide = jnp.broadcast_to(rows[:, None, :], (count, tokens, lanes))
    return wide.reshape(count * tokens, lanes)


def iotas(shape):
    return (lax.broadcasted_iota(jnp.int32, shape, 0), lax.broadcasted_iota(jnp.int32, shape, 1))


def bit_matrix(mask):
    return jnp.where(mask, 1.0, 0.0).astype(bf16)


def dot32(a, b):
    return jnp.dot(a, b, preferred_element_type=f32)


def to_parcels(rows, shape, slot_limit):
    owners, height, lanes = shape
    count = rows.shape[0] // owners
    tokens = count // slot_limit
    full = rows.shape[1] // lanes
    parts = [
        rows[:, c * lanes : (c + 1) * lanes].reshape(owners, count, lanes) for c in range(full)
    ]
    tail = rows[:, full * lanes :].reshape(owners, count, rows.shape[1] - full * lanes)
    tails = [tail[:, j * tokens : (j + 1) * tokens] for j in range(slot_limit)]
    tails += [jnp.zeros_like(tails[0])] * (slot_limit % 2)
    for j in range(0, len(tails), 2):
        parts.append(jnp.concatenate(tails[j : j + 2], axis=2))
    return jnp.concatenate(parts, axis=1).astype(bf16)


def from_parcels(parcel_ref, count, slot_limit):
    owners, height, lanes = parcel_ref.shape
    tokens = count // slot_limit
    parcels = parcel_ref[...].astype(f32)
    full = height // count
    parts = [
        parcels[:, c * count : (c + 1) * count].reshape(owners * count, lanes) for c in range(full)
    ]
    tails = []
    for j in range(slot_limit):
        first = full * count + j // 2 * tokens
        pair = parcels[:, first : first + tokens]
        tails.append(pair[:, :, j % 2 * (lanes // 2) : (j % 2 + 1) * (lanes // 2)])
    parts.append(jnp.concatenate(tails, axis=1).reshape(owners * count, lanes // 2))
    return jnp.concatenate(parts, axis=1).astype(bf16)


def asked_rows(asked_ref, slot_limit, tokens):
    owners, _, block_count = asked_ref.shape
    wanted = asked_ref[:, 0, :].astype(f32)
    row, lane = iotas((block_count, block_count))
    rank = dot32(wanted.astype(bf16), bit_matrix(row < lane))
    row, lane = iotas((owners * slot_limit, owners))
    slot = jnp.zeros((owners * slot_limit, block_count), f32)
    for j in range(slot_limit):
        level = jnp.where(rank == j, wanted, 0.0).astype(bf16)
        slot += dot32(bit_matrix(row == lane * slot_limit + j), level)
    row, lane = iotas((block_count, block_count * tokens))
    start = row * tokens
    columns = bit_matrix((lane >= start) & (lane < start + tokens))
    hot = expand(dot32(slot.astype(bf16), columns), tokens)
    row, lane = iotas(hot.shape)
    return jnp.where((row & (tokens - 1)) == (lane & (tokens - 1)), hot, 0.0).astype(bf16)


def pack_kernel(tokens, slot_limit, asked_ref, cache_ref, q_ref, g_ref, *refs):
    out_ref, q_out, g_out, rows_ref, parcel_ref, sems = refs[-6:]
    block_count = cache_ref.shape[0]
    pair = CORES * tokens
    tp = lax.axis_index("tp")
    first = pl.multiple_of(tp // CORES * pair, pair)
    copies = [
        pltpu.make_async_copy(cache_ref.at[:, pl.ds(first, pair), :], rows_ref, sems.at[0]),
        pltpu.make_async_copy(q_ref, q_out, sems.at[1]),
        pltpu.make_async_copy(g_ref, g_out, sems.at[2]),
    ]
    for copy in copies:
        copy.start()
    hot = asked_rows(asked_ref, slot_limit, tokens)
    copies[0].wait()
    rows = rows_ref[...].astype(f32)
    rows = jnp.where(tp % CORES == 0, rows[:, :tokens], rows[:, tokens:])
    rows = rows.reshape(block_count * tokens, rows_ref.shape[2]).astype(bf16)
    owners, height, lanes = out_ref.shape
    size, count = owners // PARTS, hot.shape[0] // PARTS
    for i in range(PARTS):
        part = pl.ds(i * size, size)
        moved = dot32(hot[i * count : (i + 1) * count], rows)
        parcel_ref[part] = to_parcels(moved, (size, height, lanes), slot_limit)
        copies.append(
            pltpu.make_async_copy(parcel_ref.at[part], out_ref.at[part], sems.at[3 + i])
        )
        copies[-1].start()
    for copy in copies[1:]:
        copy.wait()


def asked_kernel(tokens, slot_limit, asked_ref, out_ref):
    out_ref[...] = asked_rows(asked_ref, slot_limit, tokens).T


def owner_kernel(slot_limit, hot_ref, parcel_ref, out_ref):
    count = hot_ref.shape[1] // parcel_ref.shape[0]
    rows = from_parcels(parcel_ref, count, slot_limit)
    out_ref[...] = dot32(hot_ref[...], rows).astype(bf16)


def slot_hot(ids, tokens, lanes):
    ids = expand(jnp.broadcast_to(ids, (ids.shape[0], lanes)), tokens)
    row, lane = iotas(ids.shape)
    return bit_matrix(ids * tokens + (row & (tokens - 1)) == lane)


def unpack_kernel(tokens, slot_limit, plan_ref, parcel_ref, *refs):
    count = slot_limit * tokens
    hot = slot_hot(plan_ref[:USED, 1:2], tokens, parcel_ref.shape[0] * count)
    rows = from_parcels(parcel_ref, count, slot_limit)
    refs[-1][...] = dot32(hot, rows).astype(bf16)


def score_half(tokens, half, plan_ref, key_ref, q_refs, g_refs, p_ref, gw_ref):
    rows = p_ref.shape[2]
    heads = rows // QUERIES
    value_width = g_refs[0].shape[1]
    row, lane = iotas((plan_ref.shape[1], rows))
    start = (row - 2 - half * QUERIES) * heads
    repeat = bit_matrix((lane >= start) & (lane < start + heads))
    limit = expand(dot32(plan_ref[:USED, :].astype(f32).astype(bf16), repeat), tokens)
    token = (iotas(limit.shape)[0] & (tokens - 1)).astype(f32)
    bias = jnp.where(token <= limit, 0.0, -jnp.inf)
    for k in range(XN):
        scores = nt_dot(key_ref[...], q_refs[k][...]) * (score_scale * log2e) + bias
        peak = jnp.max(scores, axis=0, keepdims=True)
        p = jnp.exp2(scores - peak)
        gw = nt_dot(key_ref[:, :value_width], g_refs[k][...])
        p_ref[k] = p.astype(bf16)
        gw_ref[k] = gw
        total = jnp.sum(p, axis=0, keepdims=True)
        yield k, peak, total, jnp.sum(p * gw, axis=0, keepdims=True)


def own_score_kernel(tokens, plan_ref, key_ref, *refs):
    q_refs, g_refs = refs[:XN], refs[XN : 2 * XN]
    p_ref, gw_ref, stat_ref = refs[2 * XN :]
    for k, peak, total, inner in score_half(
        tokens, 0, plan_ref, key_ref, q_refs, g_refs, p_ref, gw_ref
    ):
        pad = jnp.zeros((5, peak.shape[1]), f32)
        stat_ref[k] = jnp.concatenate([peak, total, inner, pad])


def other_score_kernel(tokens, plan_ref, key_ref, *refs):
    q_refs, g_refs, own_ref = refs[:XN], refs[XN : 2 * XN], refs[2 * XN]
    p_ref, gw_ref, stat_ref = refs[2 * XN + 1 :]
    for k, peak, total, inner in score_half(
        tokens, 1, plan_ref, key_ref, q_refs, g_refs, p_ref, gw_ref
    ):
        own = own_ref[k]
        top = jnp.maximum(peak, own[0:1])
        f_own, f_other = jnp.exp2(own[0:1] - top), jnp.exp2(peak - top)
        total = own[1:2] * f_own + total * f_other
        inner = own[2:3] * f_own + inner * f_other
        pad = jnp.zeros((3, peak.shape[1]), f32)
        stat_ref[k] = jnp.concatenate([top, total, inner, f_own, f_other, pad])


def local_kernel(*refs):
    key_refs, p_refs, gw_refs = refs[:CORES], refs[CORES : 2 * CORES], refs[2 * CORES : 3 * CORES]
    stat_ref, value_ref, grad_ref = refs[3 * CORES :]
    keys_t = [key_ref[...].T for key_ref in key_refs]
    for k in range(XN):
        stats = stat_ref[k]
        inner = stats[2:3] / stats[1:2]
        value, grad = [], []
        for h in range(CORES):
            p = p_refs[h][k].astype(f32) * stats[3 + h : 4 + h]
            value.append(dot32(keys_t[h], p.astype(bf16)))
            grad.append(dot32(keys_t[h], (p * (gw_refs[h][k] - inner)).astype(bf16)))
        value_ref[k] = (value[0] + value[1]).astype(bf16)
        grad_ref[k] = (grad[0] + grad[1]).astype(bf16)


def row_stats(stat_refs, k):
    stats = [stat_refs[j][(k - j) % XN] for j in range(XN)]
    peak = functools.reduce(jnp.maximum, [s[0:1] for s in stats])
    factors = [jnp.exp2(s[0:1] - peak) for s in stats]
    total = sum(s[1:2] * f for s, f in zip(stats, factors))
    inner = sum(s[2:3] * f for s, f in zip(stats, factors)) / total
    return stats[0], inner, factors[0] / total


def key_grad_kernel(tokens, slot_limit, half, *refs):
    p_ref, gw_ref = refs[:2]
    stat_refs, q_refs, g_refs = (refs[2 + i * XN : 2 + (i + 1) * XN] for i in range(3))
    last_ref, part_ref = refs[2 + 3 * XN : 4 + 3 * XN]
    if half == 0:
        out_ref, part_out, sum_ref, sem = refs[-4:]
    else:
        out_ref, part_out, hot_ref, sum_ref, sem = refs[-5:]
    copy = pltpu.make_async_copy(part_ref, part_out, sem)
    copy.start()
    value_width = g_refs[0].shape[1]
    key_grad, value_grad = [], []
    for k in range(XN):
        mine, inner, factor = row_stats(stat_refs, k)
        factor = factor * mine[3 + half : 4 + half]
        p = p_ref[k].astype(f32)
        ds = (p * (factor * score_scale) * (gw_ref[k] - inner)).astype(bf16)
        key_grad.append(dot32(ds, q_refs[k][...]))
        value_grad.append(dot32((p * factor).astype(bf16), g_refs[k][...]))
    key_grad, value_grad = sum(key_grad), sum(value_grad)
    sum_ref[:, :value_width] = (key_grad[:, :value_width] + value_grad).astype(bf16)
    sum_ref[:, value_width:] = key_grad[:, value_width:].astype(bf16)
    if half == 0:
        hot_ref = last_ref
    else:
        hot_ref[...] = slot_hot(last_ref[:, 0:1], tokens, sum_ref.shape[0])
    rows = dot32(hot_ref[...], sum_ref[...])
    out_ref[...] = to_parcels(rows, out_ref.shape, slot_limit)
    copy.wait()


def scale_kernel(blocks, *refs):
    stat_refs, ins, outs = refs[:XN], refs[XN : XN + 2], refs[XN + 2 : -3]
    value_ref, grad_ref, sems = refs[-3:]
    copies = {
        (k, i): pltpu.make_async_copy(src.at[k], dst.at[k], sems.at[k, i])
        for k in blocks
        for i, (src, dst) in enumerate(zip(ins, (value_ref, grad_ref)))
    }
    for copy in copies.values():
        copy.start()
    for att_ref, qg_ref, k in zip(outs[::2], outs[1::2], blocks):
        copies[k, 0].wait()
        copies[k, 1].wait()
        mine, inner, factor = row_stats(stat_refs, k)
        shift = mine[2:3] / mine[1:2] - inner
        value = value_ref[k].astype(f32)
        att_ref[...] = (value[: att_ref.shape[0]] * factor).astype(bf16)
        qg = (grad_ref[k].astype(f32) + value * shift) * (factor * score_scale)
        qg_ref[...] = qg.astype(bf16)


def combine_kernel(*refs):
    for parts, out_ref in ((refs[:3], refs[6]), (refs[3:6], refs[7])):
        total = sum(part[...].astype(f32) for part in parts)
        out_ref[...] = total.astype(bf16).T


def shaped(shape, dtype=bf16):
    return jax.ShapeDtypeStruct(shape, dtype)


def call(
    kernel, out_shape, operands, name, unused=(), unused_far=(), scratch=(), far_in=0, far_out=()
):
    vmem, hbm = (pl.BlockSpec(memory_space=m) for m in (pltpu.VMEM, pltpu.HBM))
    near = len(operands) - far_in
    operands = operands[:near] + [
        pltpu.with_memory_space_constraint(x, pltpu.HBM) for x in operands[near:]
    ]
    return pl.pallas_call(
        kernel,
        out_shape=[
            pltpu.HBM(x.shape, x.dtype) if i in far_out else x for i, x in enumerate(out_shape)
        ],
        in_specs=[vmem] * near
        + [hbm] * far_in
        + [pl.BlockSpec(memory_space=pl.ANY)] * len(unused)
        + [hbm] * len(unused_far),
        out_specs=[hbm if i in far_out else vmem for i in range(len(out_shape))],
        scratch_shapes=list(scratch),
        compiler_params=pltpu.CompilerParams(vmem_limit_bytes=VMEM_LIMIT),
        name=name,
    )(
        *operands,
        *unused,
        *(pltpu.with_memory_space_constraint(x, pltpu.HBM) for x in unused_far),
    )


def slot_table(wanted, slot_limit):
    rank_within = jnp.cumsum(wanted.astype(jnp.int32), axis=1) - 1
    local_ids = jnp.arange(wanted.shape[1], dtype=jnp.int32)
    slot_range = jnp.arange(slot_limit, dtype=jnp.int32)
    matches = wanted[:, None, :] & (rank_within[:, None, :] == slot_range[None, :, None])
    present = jnp.any(matches, axis=2)
    found_ids = jnp.sum(jnp.where(matches, local_ids[None, None, :], 0), axis=2)
    return jnp.where(present, found_ids, -1).reshape(-1)


def on_device(queries, latent_cache, output_gradient, selected, positions):
    query_count, head_count, width = queries.shape
    block_count, block_size, _ = latent_cache.shape
    value_width = output_gradient.shape[2]
    owners = lax.axis_size("ctx")
    tp = lax.axis_index("tp")
    tokens = block_size // (XN * CORES)
    slot_limit = (USED - 2) // (owners - 1) + 1
    slots = owners * slot_limit
    rows = query_count * head_count
    half = USED * tokens
    keys = CORES * half
    held = block_count * tokens
    whole, tail = divmod(width, 128)
    height = (whole * slot_limit + -(-slot_limit * tail // 128)) * tokens
    parcels = (owners, height, 128)

    block_range = jnp.arange(owners * block_count, dtype=jnp.int32)
    wanted = jnp.any(selected.reshape(-1)[:, None] == block_range[None, :], axis=0)
    wanted = wanted.reshape(owners, block_count)
    asked = lax.all_to_all(
        wanted.astype(jnp.int32)[:, None, :], "ctx", split_axis=0, concat_axis=0, tiled=True
    )

    query_rows = queries.reshape(rows, width)
    grad_rows = output_gradient.reshape(rows, value_width)
    requests = slot_table(wanted, slot_limit)
    used_slot = requests >= 0
    slot_order = jnp.where(used_slot, jnp.cumsum(used_slot.astype(jnp.int32)) - 1, -1)
    compact = jnp.arange(USED, dtype=jnp.int32)
    slot_match = slot_order[None, :] == compact[:, None]
    slot_ids = jnp.arange(slots, dtype=jnp.int32)
    slot_block = slot_ids // slot_limit * block_count + requests
    picked = jnp.sum(jnp.where(slot_match, slot_ids[None, :], 0), axis=1)
    block_ids = jnp.sum(jnp.where(slot_match, slot_block[None, :], 0), axis=1)
    chosen = jnp.any(selected[None, :, :] == block_ids[:, None, None], axis=2)
    limit = jnp.where(chosen, positions[None, :] - block_ids[:, None] * block_size, -1)
    limit = jnp.clip(limit, -1, block_size - 1)
    columns = [picked[:, None], limit - tp * tokens, limit - (tp ^ 1) * tokens]
    plan = jnp.pad(jnp.concatenate(columns, axis=1), ((0, slots - USED), (0, 0)))
    plan = jnp.concatenate([slot_order[:, None], plan], axis=1)
    plan = jnp.pad(plan, ((0, 0), (0, 128 - plan.shape[1])))

    packed, q0, g0 = call(
        functools.partial(pack_kernel, tokens, slot_limit),
        [shaped(parcels), shaped((rows, width)), shaped((rows, value_width))],
        [asked, latent_cache, query_rows, grad_rows],
        "pack",
        unused=(plan,),
        scratch=[
            pltpu.VMEM((block_count, CORES * tokens, width), bf16),
            pltpu.VMEM(parcels, bf16),
            pltpu.SemaphoreType.DMA((3 + PARTS,)),
        ],
        far_in=3,
        far_out=(0,),
    )
    fetched = lax.all_to_all(packed, "ctx", 0, 0, tiled=True)

    q1, q3 = send_x(q0, 1), send_x(q0, -1)
    g1, g3 = send_x(g0, 1), send_x(g0, -1)
    q2, g2 = send_x(q1, 1), send_x(g3, -1)
    gathered = [q0, q1, q2, q3, g0, g1, g2, g3]

    (own_keys,) = call(
        functools.partial(unpack_kernel, tokens, slot_limit),
        [shaped((half, width))],
        [plan, fetched],
        "unpack",
        unused=(q1, q2, q3, g1, g2, g3),
    )
    other_keys = lax.ppermute(own_keys.reshape(USED, tokens, width), "tp", CORE_SWAP)
    other_keys = other_keys.reshape(half, width)
    score_shapes = [
        shaped((XN, half, rows)),
        shaped((XN, half, rows), f32),
        shaped((XN, 8, rows), f32),
    ]
    own_p, own_gw, own_stats = call(
        functools.partial(own_score_kernel, tokens),
        score_shapes,
        [plan, own_keys, *gathered],
        "own_scores",
    )
    other_p, other_gw, stats = call(
        functools.partial(other_score_kernel, tokens),
        score_shapes,
        [plan, other_keys, *gathered, own_stats],
        "other_scores",
    )
    all_stats = [stats] + [send_x(stats, k) for k in range(1, XN)]
    part_shape = (XN, width, rows)
    part_scratch = [
        pltpu.VMEM(part_shape, bf16),
        pltpu.VMEM(part_shape, bf16),
        pltpu.SemaphoreType.DMA((XN, 2)),
    ]
    value_part, grad_part = call(
        local_kernel,
        [shaped(part_shape)] * 2,
        [own_keys, other_keys, own_p, other_p, own_gw, other_gw, stats],
        "local",
    )

    grad_shape = shaped(parcels)
    sum_scratch = [pltpu.VMEM((half, width), bf16), pltpu.SemaphoreType.DMA(())]
    other_grad, value_part, spread_hot = call(
        functools.partial(key_grad_kernel, tokens, slot_limit, 1),
        [grad_shape, shaped(part_shape), shaped((slots * tokens, half))],
        [other_p, other_gw, *all_stats, *gathered, plan, value_part],
        "other_grads",
        far_out=(1,),
        scratch=sum_scratch,
    )
    from_core = lax.ppermute(other_grad, "tp", CORE_SWAP)
    own_grad, grad_part = call(
        functools.partial(key_grad_kernel, tokens, slot_limit, 0),
        [grad_shape, shaped(part_shape)],
        [own_p, own_gw, *all_stats, *gathered, spread_hot, grad_part],
        "own_grads",
        far_out=(1,),
        scratch=sum_scratch,
    )
    returning = (own_grad.astype(f32) + from_core.astype(f32)).astype(bf16)
    returned = lax.all_to_all(returning, "ctx", 0, 0, tiled=True)

    att, qg = {}, {}
    for blocks in ((2,), (3, 1, 0)):
        outs = call(
            functools.partial(scale_kernel, blocks),
            [shaped((value_width, rows)), shaped((width, rows))] * len(blocks),
            [*all_stats, value_part, grad_part],
            "scale",
            far_in=2,
            scratch=part_scratch,
        )
        att.update(zip(blocks, outs[::2]))
        qg.update(zip(blocks, outs[1::2]))
    att_far, qg_far = send_x(att[2], 1), send_x(qg[2], -1)
    qg_left, att_right = send_x(qg[3], 1), send_x(att[1], -1)
    att_left = (att[3].astype(f32) + att_far.astype(f32)).astype(bf16)
    qg_right = (qg[1].astype(f32) + qg_far.astype(f32)).astype(bf16)
    attended, query_grad = call(
        combine_kernel,
        [shaped((rows, value_width)), shaped((rows, width))],
        [att[0], send_x(att_left, 1), att_right, qg[0], qg_left, send_x(qg_right, -1)],
        "combine",
    )
    (asked_hot,) = call(
        functools.partial(asked_kernel, tokens, slot_limit),
        [shaped((held, slots * tokens))],
        [asked],
        "asked",
    )
    (cache_grad,) = call(
        functools.partial(owner_kernel, slot_limit),
        [shaped((held, width))],
        [asked_hot, returned],
        "owner_sum",
    )
    return (
        attended.reshape(query_count, head_count, value_width),
        query_grad.reshape(query_count, head_count, width),
        cache_grad.reshape(block_count, tokens, width),
    )


def solution(mesh):
    in_specs = (
        P("ctx", "tp", None),
        P("ctx", None, None),
        P("ctx", "tp", None),
        P("ctx", None),
        P("ctx"),
    )
    out_specs = (P("ctx", "tp", None), P("ctx", "tp", None), P("ctx", "tp", None))
    return jax.shard_map(
        on_device, mesh=mesh, in_specs=in_specs, out_specs=out_specs, check_vma=False
    )
```

```python
import functools
import math

import jax
import jax.numpy as jnp
from jax import lax
from jax.experimental import pallas as pl
from jax.experimental.pallas import tpu as pltpu
from jax.sharding import PartitionSpec as P

USED = 64
QUERIES = 16
XN = 4
CORES = 2
PARTS = 4

score_scale = 192.0 ** (-0.5)
log2e = 1.0 / math.log(2.0)
VMEM_LIMIT = 24 * 1024 * 1024
bf16 = jnp.bfloat16
f32 = jnp.float32


def x_shift(k):
    return [
        (x * CORES + c, ((x + k) % XN) * CORES + c) for x in range(XN) for c in range(CORES)
    ]


CORE_SWAP = [(t, t ^ 1) for t in range(XN * CORES)]


def send_x(value, k):
    return lax.ppermute(value, "tp", x_shift(k % XN))


def nt_dot(a, b):
    return lax.dot_general(a, b, (((1,), (1,)), ((), ())), preferred_element_type=f32)


def expand(rows, tokens):
    count, lanes = rows.shape
    wide = jnp.broadcast_to(rows[:, None, :], (count, tokens, lanes))
    return wide.reshape(count * tokens, lanes)


def iotas(shape):
    return (lax.broadcasted_iota(jnp.int32, shape, 0), lax.broadcasted_iota(jnp.int32, shape, 1))


def bit_matrix(mask):
    return jnp.where(mask, 1.0, 0.0).astype(bf16)


def dot32(a, b):
    return jnp.dot(a, b, preferred_element_type=f32)


def to_parcels(rows, shape, slot_limit):
    owners, height, lanes = shape
    count = rows.shape[0] // owners
    tokens = count // slot_limit
    full = rows.shape[1] // lanes
    parts = [
        rows[:, c * lanes : (c + 1) * lanes].reshape(owners, count, lanes) for c in range(full)
    ]
    tail = rows[:, full * lanes :].reshape(owners, count, rows.shape[1] - full * lanes)
    tails = [tail[:, j * tokens : (j + 1) * tokens] for j in range(slot_limit)]
    tails += [jnp.zeros_like(tails[0])] * (slot_limit % 2)
    for j in range(0, len(tails), 2):
        parts.append(jnp.concatenate(tails[j : j + 2], axis=2))
    return jnp.concatenate(parts, axis=1).astype(bf16)


def from_parcels(parcel_ref, count, slot_limit):
    owners, height, lanes = parcel_ref.shape
    tokens = count // slot_limit
    parcels = parcel_ref[...].astype(f32)
    full = height // count
    parts = [
        parcels[:, c * count : (c + 1) * count].reshape(owners * count, lanes) for c in range(full)
    ]
    tails = []
    for j in range(slot_limit):
        first = full * count + j // 2 * tokens
        pair = parcels[:, first : first + tokens]
        tails.append(pair[:, :, j % 2 * (lanes // 2) : (j % 2 + 1) * (lanes // 2)])
    parts.append(jnp.concatenate(tails, axis=1).reshape(owners * count, lanes // 2))
    return jnp.concatenate(parts, axis=1).astype(bf16)


def asked_rows(asked_ref, slot_limit, tokens):
    owners, _, block_count = asked_ref.shape
    wanted = asked_ref[:, 0, :].astype(f32)
    row, lane = iotas((block_count, block_count))
    rank = dot32(wanted.astype(bf16), bit_matrix(row < lane))
    row, lane = iotas((owners * slot_limit, owners))
    slot = jnp.zeros((owners * slot_limit, block_count), f32)
    for j in range(slot_limit):
        level = jnp.where(rank == j, wanted, 0.0).astype(bf16)
        slot += dot32(bit_matrix(row == lane * slot_limit + j), level)
    row, lane = iotas((block_count, block_count * tokens))
    start = row * tokens
    columns = bit_matrix((lane >= start) & (lane < start + tokens))
    hot = expand(dot32(slot.astype(bf16), columns), tokens)
    row, lane = iotas(hot.shape)
    return jnp.where((row & (tokens - 1)) == (lane & (tokens - 1)), hot, 0.0).astype(bf16)


def pack_kernel(tokens, slot_limit, asked_ref, cache_ref, q_ref, g_ref, *refs):
    out_ref, q_out, g_out, rows_ref, parcel_ref, sems = refs[-6:]
    block_count = cache_ref.shape[0]
    pair = CORES * tokens
    tp = lax.axis_index("tp")
    first = pl.multiple_of(tp // CORES * pair, pair)
    copies = [
        pltpu.make_async_copy(cache_ref.at[:, pl.ds(first, pair), :], rows_ref, sems.at[0]),
        pltpu.make_async_copy(q_ref, q_out, sems.at[1]),
        pltpu.make_async_copy(g_ref, g_out, sems.at[2]),
    ]
    for copy in copies:
        copy.start()
    hot = asked_rows(asked_ref, slot_limit, tokens)
    copies[0].wait()
    rows = rows_ref[...].astype(f32)
    rows = jnp.where(tp % CORES == 0, rows[:, :tokens], rows[:, tokens:])
    rows = rows.reshape(block_count * tokens, rows_ref.shape[2]).astype(bf16)
    owners, height, lanes = out_ref.shape
    size, count = owners // PARTS, hot.shape[0] // PARTS
    for i in range(PARTS):
        part = pl.ds(i * size, size)
        moved = dot32(hot[i * count : (i + 1) * count], rows)
        parcel_ref[part] = to_parcels(moved, (size, height, lanes), slot_limit)
        copies.append(
            pltpu.make_async_copy(parcel_ref.at[part], out_ref.at[part], sems.at[3 + i])
        )
        copies[-1].start()
    for copy in copies[1:]:
        copy.wait()


def asked_kernel(tokens, slot_limit, asked_ref, out_ref):
    out_ref[...] = asked_rows(asked_ref, slot_limit, tokens).T


def owner_kernel(slot_limit, hot_ref, parcel_ref, out_ref):
    count = hot_ref.shape[1] // parcel_ref.shape[0]
    rows = from_parcels(parcel_ref, count, slot_limit)
    out_ref[...] = dot32(hot_ref[...], rows).astype(bf16)


def slot_hot(ids, tokens, lanes):
    ids = expand(jnp.broadcast_to(ids, (ids.shape[0], lanes)), tokens)
    row, lane = iotas(ids.shape)
    return bit_matrix(ids * tokens + (row & (tokens - 1)) == lane)


def unpack_kernel(tokens, slot_limit, plan_ref, parcel_ref, *refs):
    count = slot_limit * tokens
    hot = slot_hot(plan_ref[:USED, 1:2], tokens, parcel_ref.shape[0] * count)
    rows = from_parcels(parcel_ref, count, slot_limit)
    refs[-1][...] = dot32(hot, rows).astype(bf16)


def score_half(tokens, half, plan_ref, key_ref, q_refs, g_refs, p_ref, gw_ref):
    rows = p_ref.shape[2]
    heads = rows // QUERIES
    value_width = g_refs[0].shape[1]
    row, lane = iotas((plan_ref.shape[1], rows))
    start = (row - 2 - half * QUERIES) * heads
    repeat = bit_matrix((lane >= start) & (lane < start + heads))
    limit = expand(dot32(plan_ref[:USED, :].astype(f32).astype(bf16), repeat), tokens)
    token = (iotas(limit.shape)[0] & (tokens - 1)).astype(f32)
    bias = jnp.where(token <= limit, 0.0, -jnp.inf)
    for k in range(XN):
        scores = nt_dot(key_ref[...], q_refs[k][...]) * (score_scale * log2e) + bias
        peak = jnp.max(scores, axis=0, keepdims=True)
        p = jnp.exp2(scores - peak)
        gw = nt_dot(key_ref[:, :value_width], g_refs[k][...])
        p_ref[k] = p.astype(bf16)
        gw_ref[k] = gw
        total = jnp.sum(p, axis=0, keepdims=True)
        yield k, peak, total, jnp.sum(p * gw, axis=0, keepdims=True)


def own_score_kernel(tokens, plan_ref, key_ref, *refs):
    q_refs, g_refs = refs[:XN], refs[XN : 2 * XN]
    p_ref, gw_ref, stat_ref = refs[2 * XN :]
    for k, peak, total, inner in score_half(
        tokens, 0, plan_ref, key_ref, q_refs, g_refs, p_ref, gw_ref
    ):
        pad = jnp.zeros((5, peak.shape[1]), f32)
        stat_ref[k] = jnp.concatenate([peak, total, inner, pad])


def other_score_kernel(tokens, plan_ref, key_ref, *refs):
    q_refs, g_refs, own_ref = refs[:XN], refs[XN : 2 * XN], refs[2 * XN]
    p_ref, gw_ref, stat_ref = refs[2 * XN + 1 :]
    for k, peak, total, inner in score_half(
        tokens, 1, plan_ref, key_ref, q_refs, g_refs, p_ref, gw_ref
    ):
        own = own_ref[k]
        top = jnp.maximum(peak, own[0:1])
        f_own, f_other = jnp.exp2(own[0:1] - top), jnp.exp2(peak - top)
        total = own[1:2] * f_own + total * f_other
        inner = own[2:3] * f_own + inner * f_other
        pad = jnp.zeros((3, peak.shape[1]), f32)
        stat_ref[k] = jnp.concatenate([top, total, inner, f_own, f_other, pad])


def local_kernel(*refs):
    key_refs, p_refs, gw_refs = refs[:CORES], refs[CORES : 2 * CORES], refs[2 * CORES : 3 * CORES]
    stat_ref, value_ref, grad_ref = refs[3 * CORES :]
    keys_t = [key_ref[...].T for key_ref in key_refs]
    for k in range(XN):
        stats = stat_ref[k]
        inner = stats[2:3] / stats[1:2]
        value, grad = [], []
        for h in range(CORES):
            p = p_refs[h][k].astype(f32) * stats[3 + h : 4 + h]
            value.append(dot32(keys_t[h], p.astype(bf16)))
            grad.append(dot32(keys_t[h], (p * (gw_refs[h][k] - inner)).astype(bf16)))
        value_ref[k] = (value[0] + value[1]).astype(bf16)
        grad_ref[k] = (grad[0] + grad[1]).astype(bf16)


def row_stats(stat_refs, k):
    stats = [stat_refs[j][(k - j) % XN] for j in range(XN)]
    peak = functools.reduce(jnp.maximum, [s[0:1] for s in stats])
    factors = [jnp.exp2(s[0:1] - peak) for s in stats]
    total = sum(s[1:2] * f for s, f in zip(stats, factors))
    inner = sum(s[2:3] * f for s, f in zip(stats, factors)) / total
    return stats[0], inner, factors[0] / total


def key_grad_kernel(tokens, slot_limit, half, *refs):
    p_ref, gw_ref = refs[:2]
    stat_refs, refs = refs[2 : 2 + XN], refs[2 + XN :]
    ds_ref, w_ref, sum_ref, sem = refs[-4:]
    if half == 0:
        hot_ref, q_all, g_all, part_ref, out_ref, part_out = refs[:-4]
    else:
        q_refs, g_refs = refs[:XN], refs[XN : 2 * XN]
        plan_ref, part_ref, out_ref, part_out, hot_ref, q_all, g_all = refs[2 * XN : -4]
    copy = pltpu.make_async_copy(part_ref, part_out, sem)
    copy.start()
    value_width = g_all.shape[1]
    rows = p_ref.shape[2]
    for k in range(XN):
        part = slice(k * rows, (k + 1) * rows)
        if half == 1:
            q_all[part, :] = q_refs[k][...]
            g_all[part, :] = g_refs[k][...]
        mine, inner, factor = row_stats(stat_refs, k)
        factor = factor * mine[3 + half : 4 + half]
        p = p_ref[k].astype(f32)
        ds_ref[:, part] = (p * (factor * score_scale) * (gw_ref[k] - inner)).astype(bf16)
        w_ref[:, part] = (p * factor).astype(bf16)
    key_grad = dot32(ds_ref[...], q_all[...])
    value_grad = dot32(w_ref[...], g_all[...])
    sum_ref[:, :value_width] = (key_grad[:, :value_width] + value_grad).astype(bf16)
    sum_ref[:, value_width:] = key_grad[:, value_width:].astype(bf16)
    if half == 1:
        hot_ref[...] = slot_hot(plan_ref[:, 0:1], tokens, sum_ref.shape[0])
    moved = dot32(hot_ref[...], sum_ref[...])
    out_ref[...] = to_parcels(moved, out_ref.shape, slot_limit)
    copy.wait()


def scale_kernel(blocks, *refs):
    stat_refs, ins, outs = refs[:XN], refs[XN : XN + 2], refs[XN + 2 : -3]
    value_ref, grad_ref, sems = refs[-3:]
    copies = {
        (k, i): pltpu.make_async_copy(src.at[k], dst.at[k], sems.at[k, i])
        for k in blocks
        for i, (src, dst) in enumerate(zip(ins, (value_ref, grad_ref)))
    }
    for copy in copies.values():
        copy.start()
    for att_ref, qg_ref, k in zip(outs[::2], outs[1::2], blocks):
        copies[k, 0].wait()
        copies[k, 1].wait()
        mine, inner, factor = row_stats(stat_refs, k)
        shift = mine[2:3] / mine[1:2] - inner
        value = value_ref[k].astype(f32)
        att_ref[...] = (value[: att_ref.shape[0]] * factor).astype(bf16)
        qg = (grad_ref[k].astype(f32) + value * shift) * (factor * score_scale)
        qg_ref[...] = qg.astype(bf16)


def combine_kernel(*refs):
    for parts, out_ref in ((refs[:3], refs[6]), (refs[3:6], refs[7])):
        total = sum(part[...].astype(f32) for part in parts)
        out_ref[...] = total.astype(bf16).T


def shaped(shape, dtype=bf16):
    return jax.ShapeDtypeStruct(shape, dtype)


def call(
    kernel, out_shape, operands, name, unused=(), unused_far=(), scratch=(), far_in=0, far_out=()
):
    vmem, hbm = (pl.BlockSpec(memory_space=m) for m in (pltpu.VMEM, pltpu.HBM))
    near = len(operands) - far_in
    operands = operands[:near] + [
        pltpu.with_memory_space_constraint(x, pltpu.HBM) for x in operands[near:]
    ]
    return pl.pallas_call(
        kernel,
        out_shape=[
            pltpu.HBM(x.shape, x.dtype) if i in far_out else x for i, x in enumerate(out_shape)
        ],
        in_specs=[vmem] * near
        + [hbm] * far_in
        + [pl.BlockSpec(memory_space=pl.ANY)] * len(unused)
        + [hbm] * len(unused_far),
        out_specs=[hbm if i in far_out else vmem for i in range(len(out_shape))],
        scratch_shapes=list(scratch),
        compiler_params=pltpu.CompilerParams(vmem_limit_bytes=VMEM_LIMIT),
        name=name,
    )(
        *operands,
        *unused,
        *(pltpu.with_memory_space_constraint(x, pltpu.HBM) for x in unused_far),
    )


def slot_table(wanted, slot_limit):
    rank_within = jnp.cumsum(wanted.astype(jnp.int32), axis=1) - 1
    local_ids = jnp.arange(wanted.shape[1], dtype=jnp.int32)
    slot_range = jnp.arange(slot_limit, dtype=jnp.int32)
    matches = wanted[:, None, :] & (rank_within[:, None, :] == slot_range[None, :, None])
    present = jnp.any(matches, axis=2)
    found_ids = jnp.sum(jnp.where(matches, local_ids[None, None, :], 0), axis=2)
    return jnp.where(present, found_ids, -1).reshape(-1)


def on_device(queries, latent_cache, output_gradient, selected, positions):
    query_count, head_count, width = queries.shape
    block_count, block_size, _ = latent_cache.shape
    value_width = output_gradient.shape[2]
    owners = lax.axis_size("ctx")
    tp = lax.axis_index("tp")
    tokens = block_size // (XN * CORES)
    slot_limit = (USED - 2) // (owners - 1) + 1
    slots = owners * slot_limit
    rows = query_count * head_count
    half = USED * tokens
    keys = CORES * half
    held = block_count * tokens
    whole, tail = divmod(width, 128)
    height = (whole * slot_limit + -(-slot_limit * tail // 128)) * tokens
    parcels = (owners, height, 128)

    block_range = jnp.arange(owners * block_count, dtype=jnp.int32)
    wanted = jnp.any(selected.reshape(-1)[:, None] == block_range[None, :], axis=0)
    wanted = wanted.reshape(owners, block_count)
    asked = lax.all_to_all(
        wanted.astype(jnp.int32)[:, None, :], "ctx", split_axis=0, concat_axis=0, tiled=True
    )

    query_rows = queries.reshape(rows, width)
    grad_rows = output_gradient.reshape(rows, value_width)
    requests = slot_table(wanted, slot_limit)
    used_slot = requests >= 0
    slot_order = jnp.where(used_slot, jnp.cumsum(used_slot.astype(jnp.int32)) - 1, -1)
    compact = jnp.arange(USED, dtype=jnp.int32)
    slot_match = slot_order[None, :] == compact[:, None]
    slot_ids = jnp.arange(slots, dtype=jnp.int32)
    slot_block = slot_ids // slot_limit * block_count + requests
    picked = jnp.sum(jnp.where(slot_match, slot_ids[None, :], 0), axis=1)
    block_ids = jnp.sum(jnp.where(slot_match, slot_block[None, :], 0), axis=1)
    chosen = jnp.any(selected[None, :, :] == block_ids[:, None, None], axis=2)
    limit = jnp.where(chosen, positions[None, :] - block_ids[:, None] * block_size, -1)
    limit = jnp.clip(limit, -1, block_size - 1)
    columns = [picked[:, None], limit - tp * tokens, limit - (tp ^ 1) * tokens]
    plan = jnp.pad(jnp.concatenate(columns, axis=1), ((0, slots - USED), (0, 0)))
    plan = jnp.concatenate([slot_order[:, None], plan], axis=1)
    plan = jnp.pad(plan, ((0, 0), (0, 128 - plan.shape[1])))

    packed, q0, g0 = call(
        functools.partial(pack_kernel, tokens, slot_limit),
        [shaped(parcels), shaped((rows, width)), shaped((rows, value_width))],
        [asked, latent_cache, query_rows, grad_rows],
        "pack",
        unused=(plan,),
        scratch=[
            pltpu.VMEM((block_count, CORES * tokens, width), bf16),
            pltpu.VMEM(parcels, bf16),
            pltpu.SemaphoreType.DMA((3 + PARTS,)),
        ],
        far_in=3,
        far_out=(0,),
    )
    fetched = lax.all_to_all(packed, "ctx", 0, 0, tiled=True)

    q1, q3 = send_x(q0, 1), send_x(q0, -1)
    g1, g3 = send_x(g0, 1), send_x(g0, -1)
    q2, g2 = send_x(q1, 1), send_x(g3, -1)
    gathered = [q0, q1, q2, q3, g0, g1, g2, g3]

    (own_keys,) = call(
        functools.partial(unpack_kernel, tokens, slot_limit),
        [shaped((half, width))],
        [plan, fetched],
        "unpack",
        unused=(q1, q2, q3, g1, g2, g3),
    )
    other_keys = lax.ppermute(own_keys.reshape(USED, tokens, width), "tp", CORE_SWAP)
    other_keys = other_keys.reshape(half, width)
    score_shapes = [
        shaped((XN, half, rows)),
        shaped((XN, half, rows), f32),
        shaped((XN, 8, rows), f32),
    ]
    own_p, own_gw, own_stats = call(
        functools.partial(own_score_kernel, tokens),
        score_shapes,
        [plan, own_keys, *gathered],
        "own_scores",
    )
    other_p, other_gw, stats = call(
        functools.partial(other_score_kernel, tokens),
        score_shapes,
        [plan, other_keys, *gathered, own_stats],
        "other_scores",
    )
    all_stats = [stats] + [send_x(stats, k) for k in range(1, XN)]
    part_shape = (XN, width, rows)
    part_scratch = [
        pltpu.VMEM(part_shape, bf16),
        pltpu.VMEM(part_shape, bf16),
        pltpu.SemaphoreType.DMA((XN, 2)),
    ]
    value_part, grad_part = call(
        local_kernel,
        [shaped(part_shape)] * 2,
        [own_keys, other_keys, own_p, other_p, own_gw, other_gw, stats],
        "local",
    )

    grad_shape = shaped(parcels)
    sum_scratch = [
        pltpu.VMEM((half, XN * rows), bf16),
        pltpu.VMEM((half, XN * rows), bf16),
        pltpu.VMEM((half, width), bf16),
        pltpu.SemaphoreType.DMA(()),
    ]
    other_grad, value_part, spread_hot, q_all, g_all = call(
        functools.partial(key_grad_kernel, tokens, slot_limit, 1),
        [
            grad_shape,
            shaped(part_shape),
            shaped((slots * tokens, half)),
            shaped((XN * rows, width)),
            shaped((XN * rows, value_width)),
        ],
        [other_p, other_gw, *all_stats, *gathered, plan, value_part],
        "other_grads",
        far_out=(1,),
        scratch=sum_scratch,
    )
    from_core = lax.ppermute(other_grad, "tp", CORE_SWAP)
    own_grad, grad_part = call(
        functools.partial(key_grad_kernel, tokens, slot_limit, 0),
        [grad_shape, shaped(part_shape)],
        [own_p, own_gw, *all_stats, spread_hot, q_all, g_all, grad_part],
        "own_grads",
        far_out=(1,),
        scratch=sum_scratch,
    )
    returning = (own_grad.astype(f32) + from_core.astype(f32)).astype(bf16)
    returned = lax.all_to_all(returning, "ctx", 0, 0, tiled=True)

    att, qg = {}, {}
    for blocks in ((2,), (3, 1, 0)):
        outs = call(
            functools.partial(scale_kernel, blocks),
            [shaped((value_width, rows)), shaped((width, rows))] * len(blocks),
            [*all_stats, value_part, grad_part],
            "scale",
            far_in=2,
            scratch=part_scratch,
        )
        att.update(zip(blocks, outs[::2]))
        qg.update(zip(blocks, outs[1::2]))
    att_far, qg_far = send_x(att[2], 1), send_x(qg[2], -1)
    qg_left, att_right = send_x(qg[3], 1), send_x(att[1], -1)
    att_left = (att[3].astype(f32) + att_far.astype(f32)).astype(bf16)
    qg_right = (qg[1].astype(f32) + qg_far.astype(f32)).astype(bf16)
    attended, query_grad = call(
        combine_kernel,
        [shaped((rows, value_width)), shaped((rows, width))],
        [att[0], send_x(att_left, 1), att_right, qg[0], qg_left, send_x(qg_right, -1)],
        "combine",
    )
    (asked_hot,) = call(
        functools.partial(asked_kernel, tokens, slot_limit),
        [shaped((held, slots * tokens))],
        [asked],
        "asked",
    )
    (cache_grad,) = call(
        functools.partial(owner_kernel, slot_limit),
        [shaped((held, width))],
        [asked_hot, returned],
        "owner_sum",
    )
    return (
        attended.reshape(query_count, head_count, value_width),
        query_grad.reshape(query_count, head_count, width),
        cache_grad.reshape(block_count, tokens, width),
    )


def solution(mesh):
    in_specs = (
        P("ctx", "tp", None),
        P("ctx", None, None),
        P("ctx", "tp", None),
        P("ctx", None),
        P("ctx"),
    )
    out_specs = (P("ctx", "tp", None), P("ctx", "tp", None), P("ctx", "tp", None))
    return jax.shard_map(
        on_device, mesh=mesh, in_specs=in_specs, out_specs=out_specs, check_vma=False
    )
```

```python
import functools
import math

import jax
import jax.numpy as jnp
from jax import lax
from jax.experimental import pallas as pl
from jax.experimental.pallas import tpu as pltpu
from jax.sharding import PartitionSpec as P

USED = 64
QUERIES = 16
XN = 4
CORES = 2
PARTS = 4

score_scale = 192.0 ** (-0.5)
log2e = 1.0 / math.log(2.0)
VMEM_LIMIT = 24 * 1024 * 1024
bf16 = jnp.bfloat16
f32 = jnp.float32


def x_shift(k):
    return [
        (x * CORES + c, ((x + k) % XN) * CORES + c) for x in range(XN) for c in range(CORES)
    ]


CORE_SWAP = [(t, t ^ 1) for t in range(XN * CORES)]


def send_x(value, k):
    return lax.ppermute(value, "tp", x_shift(k % XN))


def nt_dot(a, b):
    return lax.dot_general(a, b, (((1,), (1,)), ((), ())), preferred_element_type=f32)


def expand(rows, tokens):
    count, lanes = rows.shape
    wide = jnp.broadcast_to(rows[:, None, :], (count, tokens, lanes))
    return wide.reshape(count * tokens, lanes)


def iotas(shape):
    return (lax.broadcasted_iota(jnp.int32, shape, 0), lax.broadcasted_iota(jnp.int32, shape, 1))


def bit_matrix(mask):
    return jnp.where(mask, 1.0, 0.0).astype(bf16)


def dot32(a, b):
    return jnp.dot(a, b, preferred_element_type=f32)


def to_parcels(rows, shape, slot_limit):
    owners, height, lanes = shape
    count = rows.shape[0] // owners
    tokens = count // slot_limit
    full = rows.shape[1] // lanes
    parts = [
        rows[:, c * lanes : (c + 1) * lanes].reshape(owners, count, lanes) for c in range(full)
    ]
    tail = rows[:, full * lanes :].reshape(owners, count, rows.shape[1] - full * lanes)
    tails = [tail[:, j * tokens : (j + 1) * tokens] for j in range(slot_limit)]
    tails += [jnp.zeros_like(tails[0])] * (slot_limit % 2)
    for j in range(0, len(tails), 2):
        parts.append(jnp.concatenate(tails[j : j + 2], axis=2))
    return jnp.concatenate(parts, axis=1).astype(bf16)


def from_parcels(parcel_ref, count, slot_limit):
    owners, height, lanes = parcel_ref.shape
    tokens = count // slot_limit
    parcels = parcel_ref[...].astype(f32)
    full = height // count
    parts = [
        parcels[:, c * count : (c + 1) * count].reshape(owners * count, lanes) for c in range(full)
    ]
    tails = []
    for j in range(slot_limit):
        first = full * count + j // 2 * tokens
        pair = parcels[:, first : first + tokens]
        tails.append(pair[:, :, j % 2 * (lanes // 2) : (j % 2 + 1) * (lanes // 2)])
    parts.append(jnp.concatenate(tails, axis=1).reshape(owners * count, lanes // 2))
    return jnp.concatenate(parts, axis=1).astype(bf16)


def asked_rows(asked_ref, slot_limit, tokens):
    owners, _, block_count = asked_ref.shape
    wanted = asked_ref[:, 0, :].astype(f32)
    row, lane = iotas((block_count, block_count))
    rank = dot32(wanted.astype(bf16), bit_matrix(row < lane))
    row, lane = iotas((owners * slot_limit, owners))
    slot = jnp.zeros((owners * slot_limit, block_count), f32)
    for j in range(slot_limit):
        level = jnp.where(rank == j, wanted, 0.0).astype(bf16)
        slot += dot32(bit_matrix(row == lane * slot_limit + j), level)
    row, lane = iotas((block_count, block_count * tokens))
    start = row * tokens
    columns = bit_matrix((lane >= start) & (lane < start + tokens))
    hot = expand(dot32(slot.astype(bf16), columns), tokens)
    row, lane = iotas(hot.shape)
    return jnp.where((row & (tokens - 1)) == (lane & (tokens - 1)), hot, 0.0).astype(bf16)


def pack_kernel(tokens, slot_limit, asked_ref, cache_ref, q_ref, g_ref, *refs):
    out_ref, q_out, g_out, rows_ref, parcel_ref, sems = refs[-6:]
    block_count = cache_ref.shape[0]
    pair = CORES * tokens
    tp = lax.axis_index("tp")
    first = pl.multiple_of(tp // CORES * pair, pair)
    copies = [
        pltpu.make_async_copy(cache_ref.at[:, pl.ds(first, pair), :], rows_ref, sems.at[0]),
        pltpu.make_async_copy(q_ref, q_out, sems.at[1]),
        pltpu.make_async_copy(g_ref, g_out, sems.at[2]),
    ]
    for copy in copies:
        copy.start()
    hot = asked_rows(asked_ref, slot_limit, tokens)
    copies[0].wait()
    rows = rows_ref[...].astype(f32)
    rows = jnp.where(tp % CORES == 0, rows[:, :tokens], rows[:, tokens:])
    rows = rows.reshape(block_count * tokens, rows_ref.shape[2]).astype(bf16)
    owners, height, lanes = out_ref.shape
    size, count = owners // PARTS, hot.shape[0] // PARTS
    for i in range(PARTS):
        part = pl.ds(i * size, size)
        moved = dot32(hot[i * count : (i + 1) * count], rows)
        parcel_ref[part] = to_parcels(moved, (size, height, lanes), slot_limit)
        copies.append(
            pltpu.make_async_copy(parcel_ref.at[part], out_ref.at[part], sems.at[3 + i])
        )
        copies[-1].start()
    for copy in copies[1:]:
        copy.wait()


def asked_kernel(tokens, slot_limit, asked_ref, out_ref):
    out_ref[...] = asked_rows(asked_ref, slot_limit, tokens).T


def owner_kernel(slot_limit, hot_ref, parcel_ref, out_ref):
    count = hot_ref.shape[1] // parcel_ref.shape[0]
    rows = from_parcels(parcel_ref, count, slot_limit)
    out_ref[...] = dot32(hot_ref[...], rows).astype(bf16)


def slot_hot(ids, tokens, lanes):
    ids = expand(jnp.broadcast_to(ids, (ids.shape[0], lanes)), tokens)
    row, lane = iotas(ids.shape)
    return bit_matrix(ids * tokens + (row & (tokens - 1)) == lane)


def unpack_kernel(tokens, slot_limit, plan_ref, parcel_ref, *refs):
    count = slot_limit * tokens
    hot = slot_hot(plan_ref[:USED, 1:2], tokens, parcel_ref.shape[0] * count)
    rows = from_parcels(parcel_ref, count, slot_limit)
    refs[-1][...] = dot32(hot, rows).astype(bf16)


def score_half(tokens, half, plan_ref, key_ref, q_refs, g_refs, p_ref, gw_ref):
    rows = p_ref.shape[2]
    heads = rows // QUERIES
    value_width = g_refs[0].shape[1]
    row, lane = iotas((plan_ref.shape[1], rows))
    start = (row - 2 - half * QUERIES) * heads
    repeat = bit_matrix((lane >= start) & (lane < start + heads))
    limit = expand(dot32(plan_ref[:USED, :].astype(f32).astype(bf16), repeat), tokens)
    token = (iotas(limit.shape)[0] & (tokens - 1)).astype(f32)
    bias = jnp.where(token <= limit, 0.0, -jnp.inf)
    for k in range(XN):
        scores = nt_dot(key_ref[...], q_refs[k][...]) * (score_scale * log2e) + bias
        peak = jnp.max(scores, axis=0, keepdims=True)
        p = jnp.exp2(scores - peak)
        gw = nt_dot(key_ref[:, :value_width], g_refs[k][...])
        p_ref[k] = p.astype(bf16)
        gw_ref[k] = gw
        total = jnp.sum(p, axis=0, keepdims=True)
        yield k, peak, total, jnp.sum(p * gw, axis=0, keepdims=True)


def own_score_kernel(tokens, plan_ref, key_ref, *refs):
    q_refs, g_refs = refs[:XN], refs[XN : 2 * XN]
    p_ref, gw_ref, stat_ref = refs[2 * XN :]
    for k, peak, total, inner in score_half(
        tokens, 0, plan_ref, key_ref, q_refs, g_refs, p_ref, gw_ref
    ):
        pad = jnp.zeros((5, peak.shape[1]), f32)
        stat_ref[k] = jnp.concatenate([peak, total, inner, pad])


def other_score_kernel(tokens, plan_ref, key_ref, *refs):
    q_refs, g_refs, own_ref = refs[:XN], refs[XN : 2 * XN], refs[2 * XN]
    p_ref, gw_ref, stat_ref = refs[2 * XN + 1 :]
    for k, peak, total, inner in score_half(
        tokens, 1, plan_ref, key_ref, q_refs, g_refs, p_ref, gw_ref
    ):
        own = own_ref[k]
        top = jnp.maximum(peak, own[0:1])
        f_own, f_other = jnp.exp2(own[0:1] - top), jnp.exp2(peak - top)
        total = own[1:2] * f_own + total * f_other
        inner = own[2:3] * f_own + inner * f_other
        pad = jnp.zeros((3, peak.shape[1]), f32)
        stat_ref[k] = jnp.concatenate([top, total, inner, f_own, f_other, pad])


def local_kernel(*refs):
    key_refs, p_refs, gw_refs = refs[:CORES], refs[CORES : 2 * CORES], refs[2 * CORES : 3 * CORES]
    stat_ref, value_ref, grad_ref = refs[3 * CORES :]
    keys_t = [key_ref[...].T for key_ref in key_refs]
    for k in range(XN):
        stats = stat_ref[k]
        inner = stats[2:3] / stats[1:2]
        value, grad = [], []
        for h in range(CORES):
            p = p_refs[h][k].astype(f32) * stats[3 + h : 4 + h]
            value.append(dot32(keys_t[h], p.astype(bf16)))
            grad.append(dot32(keys_t[h], (p * (gw_refs[h][k] - inner)).astype(bf16)))
        value_ref[k] = (value[0] + value[1]).astype(bf16)
        grad_ref[k] = (grad[0] + grad[1]).astype(bf16)


def row_stats(stat_refs, k):
    stats = [stat_refs[j][(k - j) % XN] for j in range(XN)]
    peak = functools.reduce(jnp.maximum, [s[0:1] for s in stats])
    factors = [jnp.exp2(s[0:1] - peak) for s in stats]
    total = sum(s[1:2] * f for s, f in zip(stats, factors))
    inner = sum(s[2:3] * f for s, f in zip(stats, factors)) / total
    return stats[0], inner, factors[0] / total


def key_grad_kernel(tokens, slot_limit, half, *refs):
    p_ref, gw_ref = refs[:2]
    stat_refs, refs = refs[2 : 2 + XN], refs[2 + XN :]
    ds_ref, w_ref, sum_ref, sem = refs[-4:]
    if half == 0:
        hot_ref, q_all, g_all, part_ref, out_ref, part_out = refs[:-4]
    else:
        q_refs, g_refs = refs[:XN], refs[XN : 2 * XN]
        plan_ref, part_ref, out_ref, part_out, hot_ref, q_all, g_all = refs[2 * XN : -4]
    copy = pltpu.make_async_copy(part_ref, part_out, sem)
    copy.start()
    value_width = g_all.shape[1]
    rows = p_ref.shape[2]
    for k in range(XN):
        part = slice(k * rows, (k + 1) * rows)
        if half == 1:
            q_all[part, :] = q_refs[k][...]
            g_all[part, :] = g_refs[k][...]
        mine, inner, factor = row_stats(stat_refs, k)
        factor = factor * mine[3 + half : 4 + half]
        p = p_ref[k].astype(f32)
        ds_ref[:, part] = (p * (factor * score_scale) * (gw_ref[k] - inner)).astype(bf16)
        w_ref[:, part] = (p * factor).astype(bf16)
    key_grad = dot32(ds_ref[...], q_all[...])
    value_grad = dot32(w_ref[...], g_all[...])
    sum_ref[:, :value_width] = (key_grad[:, :value_width] + value_grad).astype(bf16)
    sum_ref[:, value_width:] = key_grad[:, value_width:].astype(bf16)
    if half == 1:
        hot_ref[...] = slot_hot(plan_ref[:, 0:1], tokens, sum_ref.shape[0])
    moved = dot32(hot_ref[...], sum_ref[...])
    out_ref[...] = to_parcels(moved, out_ref.shape, slot_limit)
    copy.wait()


def scale_kernel(blocks, *refs):
    stat_refs, ins, outs = refs[:XN], refs[XN : XN + 2], refs[XN + 2 : -3]
    value_ref, grad_ref, sems = refs[-3:]
    copies = {
        (k, i): pltpu.make_async_copy(src.at[k], dst.at[k], sems.at[k, i])
        for k in blocks
        for i, (src, dst) in enumerate(zip(ins, (value_ref, grad_ref)))
    }
    for copy in copies.values():
        copy.start()
    for att_ref, qg_ref, k in zip(outs[::2], outs[1::2], blocks):
        copies[k, 0].wait()
        copies[k, 1].wait()
        mine, inner, factor = row_stats(stat_refs, k)
        shift = mine[2:3] / mine[1:2] - inner
        value = value_ref[k].astype(f32)
        att_ref[...] = (value[: att_ref.shape[0]] * factor).astype(bf16)
        qg = (grad_ref[k].astype(f32) + value * shift) * (factor * score_scale)
        qg_ref[...] = qg.astype(bf16)


def combine_kernel(*refs):
    for parts, out_ref in ((refs[:3], refs[6]), (refs[3:6], refs[7])):
        total = sum(part[...].astype(f32) for part in parts)
        out_ref[...] = total.astype(bf16).T


def shaped(shape, dtype=bf16):
    return jax.ShapeDtypeStruct(shape, dtype)


def call(
    kernel, out_shape, operands, name, unused=(), unused_far=(), scratch=(), far_in=0, far_out=()
):
    vmem, hbm = (pl.BlockSpec(memory_space=m) for m in (pltpu.VMEM, pltpu.HBM))
    near = len(operands) - far_in
    operands = operands[:near] + [
        pltpu.with_memory_space_constraint(x, pltpu.HBM) for x in operands[near:]
    ]
    return pl.pallas_call(
        kernel,
        out_shape=[
            pltpu.HBM(x.shape, x.dtype) if i in far_out else x for i, x in enumerate(out_shape)
        ],
        in_specs=[vmem] * near
        + [hbm] * far_in
        + [pl.BlockSpec(memory_space=pl.ANY)] * len(unused)
        + [hbm] * len(unused_far),
        out_specs=[hbm if i in far_out else vmem for i in range(len(out_shape))],
        scratch_shapes=list(scratch),
        compiler_params=pltpu.CompilerParams(vmem_limit_bytes=VMEM_LIMIT),
        name=name,
    )(
        *operands,
        *unused,
        *(pltpu.with_memory_space_constraint(x, pltpu.HBM) for x in unused_far),
    )


def slot_table(wanted, slot_limit):
    rank_within = jnp.cumsum(wanted.astype(jnp.int32), axis=1) - 1
    local_ids = jnp.arange(wanted.shape[1], dtype=jnp.int32)
    slot_range = jnp.arange(slot_limit, dtype=jnp.int32)
    matches = wanted[:, None, :] & (rank_within[:, None, :] == slot_range[None, :, None])
    present = jnp.any(matches, axis=2)
    found_ids = jnp.sum(jnp.where(matches, local_ids[None, None, :], 0), axis=2)
    return jnp.where(present, found_ids, -1).reshape(-1)


def on_device(queries, latent_cache, output_gradient, selected, positions):
    query_count, head_count, width = queries.shape
    block_count, block_size, _ = latent_cache.shape
    value_width = output_gradient.shape[2]
    owners = lax.axis_size("ctx")
    tp = lax.axis_index("tp")
    tokens = block_size // (XN * CORES)
    slot_limit = (USED - 2) // (owners - 1) + 1
    slots = owners * slot_limit
    rows = query_count * head_count
    half = USED * tokens
    keys = CORES * half
    held = block_count * tokens
    whole, tail = divmod(width, 128)
    height = (whole * slot_limit + -(-slot_limit * tail // 128)) * tokens
    parcels = (owners, height, 128)

    block_range = jnp.arange(owners * block_count, dtype=jnp.int32)
    wanted = jnp.any(selected.reshape(-1)[:, None] == block_range[None, :], axis=0)
    wanted = wanted.reshape(owners, block_count)
    asked = lax.all_to_all(
        wanted.astype(jnp.int32)[:, None, :], "ctx", split_axis=0, concat_axis=0, tiled=True
    )

    query_rows = queries.reshape(rows, width)
    grad_rows = output_gradient.reshape(rows, value_width)
    requests = slot_table(wanted, slot_limit)
    used_slot = requests >= 0
    slot_order = jnp.where(used_slot, jnp.cumsum(used_slot.astype(jnp.int32)) - 1, -1)
    compact = jnp.arange(USED, dtype=jnp.int32)
    slot_match = slot_order[None, :] == compact[:, None]
    slot_ids = jnp.arange(slots, dtype=jnp.int32)
    slot_block = slot_ids // slot_limit * block_count + requests
    picked = jnp.sum(jnp.where(slot_match, slot_ids[None, :], 0), axis=1)
    block_ids = jnp.sum(jnp.where(slot_match, slot_block[None, :], 0), axis=1)
    chosen = jnp.any(selected[None, :, :] == block_ids[:, None, None], axis=2)
    limit = jnp.where(chosen, positions[None, :] - block_ids[:, None] * block_size, -1)
    limit = jnp.clip(limit, -1, block_size - 1)
    columns = [picked[:, None], limit - tp * tokens, limit - (tp ^ 1) * tokens]
    plan = jnp.pad(jnp.concatenate(columns, axis=1), ((0, slots - USED), (0, 0)))
    plan = jnp.concatenate([slot_order[:, None], plan], axis=1)
    plan = jnp.pad(plan, ((0, 0), (0, 128 - plan.shape[1])))

    packed, q0, g0 = call(
        functools.partial(pack_kernel, tokens, slot_limit),
        [shaped(parcels), shaped((rows, width)), shaped((rows, value_width))],
        [asked, latent_cache, query_rows, grad_rows],
        "pack",
        unused=(plan,),
        scratch=[
            pltpu.VMEM((block_count, CORES * tokens, width), bf16),
            pltpu.VMEM(parcels, bf16),
            pltpu.SemaphoreType.DMA((3 + PARTS,)),
        ],
        far_in=3,
        far_out=(0,),
    )
    fetched = lax.all_to_all(packed, "ctx", 0, 0, tiled=True)

    q1, q3 = send_x(q0, 1), send_x(q0, -1)
    g1, g3 = send_x(g0, 1), send_x(g0, -1)
    q2, g2 = send_x(q1, 1), send_x(g3, -1)
    gathered = [q0, q1, q2, q3, g0, g1, g2, g3]

    (own_keys,) = call(
        functools.partial(unpack_kernel, tokens, slot_limit),
        [shaped((half, width))],
        [plan, fetched],
        "unpack",
        unused=(q1, q2, q3, g1, g2, g3),
    )
    other_keys = lax.ppermute(own_keys.reshape(USED, tokens, width), "tp", CORE_SWAP)
    other_keys = other_keys.reshape(half, width)
    score_shapes = [
        shaped((XN, half, rows)),
        shaped((XN, half, rows), f32),
        shaped((XN, 8, rows), f32),
    ]
    own_p, own_gw, own_stats = call(
        functools.partial(own_score_kernel, tokens),
        score_shapes,
        [plan, own_keys, *gathered],
        "own_scores",
    )
    other_p, other_gw, stats = call(
        functools.partial(other_score_kernel, tokens),
        score_shapes,
        [plan, other_keys, *gathered, own_stats],
        "other_scores",
    )
    all_stats = [stats] + [send_x(stats, k) for k in range(1, XN)]
    part_shape = (XN, width, rows)
    part_scratch = [
        pltpu.VMEM(part_shape, bf16),
        pltpu.VMEM(part_shape, bf16),
        pltpu.SemaphoreType.DMA((XN, 2)),
    ]
    value_part, grad_part = call(
        local_kernel,
        [shaped(part_shape)] * 2,
        [own_keys, other_keys, own_p, other_p, own_gw, other_gw, stats],
        "local",
    )

    grad_shape = shaped(parcels)
    sum_scratch = [
        pltpu.VMEM((half, XN * rows), bf16),
        pltpu.VMEM((half, XN * rows), bf16),
        pltpu.VMEM((half, width), bf16),
        pltpu.SemaphoreType.DMA(()),
    ]
    other_grad, value_part, spread_hot, q_all, g_all = call(
        functools.partial(key_grad_kernel, tokens, slot_limit, 1),
        [
            grad_shape,
            shaped(part_shape),
            shaped((slots * tokens, half)),
            shaped((XN * rows, width)),
            shaped((XN * rows, value_width)),
        ],
        [other_p, other_gw, *all_stats, *gathered, plan, value_part],
        "other_grads",
        far_out=(1,),
        scratch=sum_scratch,
    )
    from_core = lax.ppermute(other_grad, "tp", CORE_SWAP)
    own_grad, grad_part = call(
        functools.partial(key_grad_kernel, tokens, slot_limit, 0),
        [grad_shape, shaped(part_shape)],
        [own_p, own_gw, *all_stats, spread_hot, q_all, g_all, grad_part],
        "own_grads",
        far_out=(1,),
        scratch=sum_scratch,
    )
    returning = (own_grad.astype(f32) + from_core.astype(f32)).astype(bf16)
    returned = lax.all_to_all(returning, "ctx", 0, 0, tiled=True)

    att, qg = {}, {}
    for blocks in ((2,), (3, 1), (0,)):
        outs = call(
            functools.partial(scale_kernel, blocks),
            [shaped((value_width, rows)), shaped((width, rows))] * len(blocks),
            [*all_stats, value_part, grad_part],
            "scale",
            far_in=2,
            scratch=part_scratch,
        )
        att.update(zip(blocks, outs[::2]))
        qg.update(zip(blocks, outs[1::2]))
    att_far, qg_far = send_x(att[2], 1), send_x(qg[2], -1)
    qg_left, att_right = send_x(qg[3], 1), send_x(att[1], -1)
    att_left = (att[3].astype(f32) + att_far.astype(f32)).astype(bf16)
    qg_right = (qg[1].astype(f32) + qg_far.astype(f32)).astype(bf16)
    attended, query_grad = call(
        combine_kernel,
        [shaped((rows, value_width)), shaped((rows, width))],
        [att[0], send_x(att_left, 1), att_right, qg[0], qg_left, send_x(qg_right, -1)],
        "combine",
    )
    (asked_hot,) = call(
        functools.partial(asked_kernel, tokens, slot_limit),
        [shaped((held, slots * tokens))],
        [asked],
        "asked",
    )
    (cache_grad,) = call(
        functools.partial(owner_kernel, slot_limit),
        [shaped((held, width))],
        [asked_hot, returned],
        "owner_sum",
    )
    return (
        attended.reshape(query_count, head_count, value_width),
        query_grad.reshape(query_count, head_count, width),
        cache_grad.reshape(block_count, tokens, width),
    )


def solution(mesh):
    in_specs = (
        P("ctx", "tp", None),
        P("ctx", None, None),
        P("ctx", "tp", None),
        P("ctx", None),
        P("ctx"),
    )
    out_specs = (P("ctx", "tp", None), P("ctx", "tp", None), P("ctx", "tp", None))
    return jax.shard_map(
        on_device, mesh=mesh, in_specs=in_specs, out_specs=out_specs, check_vma=False
    )
```
